32 devices in a mesh: blk: 8 (over y, x, core), rep: 4 (over z).
Axes of the slice: x: 2, y: 2, z: 4, core: 2. Of those that a mesh axis runs over, the one named last changes fastest.
Arguments:
- features: bfloat16 [4096, 256], P(('blk', 'rep')), may hold values from -6 to 6
- weight: bfloat16 [256, 256], replicated, may hold values from -0.375 to 0.375
- cotangent: bfloat16 [4096, 256], P(('blk', 'rep')), may hold values from -6 to 6
- block_rows: int32 [8, 8, 4, 2], P('blk', None, 'rep'), may hold values from 0 to 3, as said below
- block_counts: int32 [8, 8, 4], P('blk', None, 'rep'), may hold values from 1 to 2, as said below
- block_values: bfloat16 [8, 8, 4, 128, 256], P('blk', None, 'rep'), as said below
Outputs:
- activation: bfloat16 [4096, 256], P(('blk', 'rep'))
- grad_weight: float32 [256, 256], replicated
- grad_features: bfloat16 [4096, 256], P(('blk', 'rep'))
The draws below stay inside these ranges and needn't reach their ends.
Inputs may be any that keep to these rules, and one draw needn't show every extreme that they name: `block_rows`: within one block row, column block and column set the 2 row-block numbers are distinct; slots at or beyond the count hold valid numbers and are not part of A. block_counts[i, j, r] does not depend on r, equals block_counts[j, i, r], and block_counts[i, i, r] = 2. `block_values`: Positive, and the adjacency A built from the three adjacency arguments is exactly symmetric.
All inputs are finite; a program needn't handle non-finite values.
Results may differ from the reference program's by a relative error of at most 0.017.
Values may be sent and summed in bfloat16 or wider, within the bound.
No kernel may reach another device: no remote copies, remote signals or barrier semaphores. Data moves between devices by JAX's collectives and lax.ppermute only.
A program may use at most 64 MiB of HBM per device.

```python
import math
import jax
import jax.numpy as jnp
from jax import lax

FEAT = 256
BLOCK = 128
SLOTS = 2
SUBS = 4
SLABS = 8
NODES = 4096


def adjacency_plan(key):
    order_key = jax.random.fold_in(key, 101)
    center_key = jax.random.fold_in(key, 102)
    sub_iota = jnp.arange(SUBS, dtype=jnp.int32)
    scores = jax.random.randint(order_key, (SLABS, SUBS), 0, 1 << 20) * SUBS + sub_iota[None, :]
    order = jnp.argsort(scores, axis=1, stable=True).astype(jnp.int32)
    inverse = jnp.argsort(order, axis=1, stable=True).astype(jnp.int32)
    block_iota = jnp.arange(SLABS, dtype=jnp.int32)
    slot_iota = jnp.arange(SLOTS, dtype=jnp.int32)
    slot_place = (slot_iota[None, None, None, :] - inverse[None, :, :, None]) % SUBS
    slot_place = jnp.broadcast_to(slot_place, (SLABS, SLABS, SUBS, SLOTS))
    rows = order[block_iota[:, None, None, None], slot_place]
    centers = jax.random.randint(center_key, (SLABS,), 0, 4) == 0
    linked = centers[:, None] | centers[None, :] | (block_iota[:, None] == block_iota[None, :])
    counts = jnp.where(linked, SLOTS, 1).astype(jnp.int32)
    return (rows.astype(jnp.int32), counts)


def draw_block_rows(key, part):
    rows, counts = adjacency_plan(key)
    return rows


def draw_block_counts(key, part):
    rows, counts = adjacency_plan(key)
    return jnp.broadcast_to(counts[:, :, None], (SLABS, SLABS, SUBS)).astype(jnp.int32)


def draw_block_values(key, part):
    own_key = jax.random.fold_in(key, 3)
    rows, counts = adjacency_plan(key)
    raw = jax.random.uniform(own_key, (SLABS, SLABS, SUBS, SLOTS, BLOCK, BLOCK), jnp.float32, 0.1, 1.0)
    block_iota = jnp.arange(SLABS, dtype=jnp.int32)
    slot_iota = jnp.arange(SLOTS, dtype=jnp.int32)
    mirror = raw[block_iota[None, :, None, None], block_iota[:, None, None, None], rows, slot_iota[None, None, None, :]]
    mirror = jnp.swapaxes(mirror, -1, -2)
    factor = 0.5 / math.sqrt(0.7 * BLOCK * SLABS)
    values = (raw + mirror) * factor
    values = values.transpose(0, 1, 2, 4, 3, 5).reshape(SLABS, SLABS, SUBS, BLOCK, SLOTS * BLOCK)
    return values.astype(jnp.bfloat16)


def block_levels(key, shape, pieces, low, largest):
    factor_of, own = 1.0, jax.random.fold_in(key, 6)
    for position, blocks in pieces:
        draws = jnp.exp(jax.random.uniform(jax.random.fold_in(own, position), (blocks,), jnp.float32, low / len(pieces), largest / len(pieces)))
        factor_of = factor_of * jnp.repeat(draws, shape[position] // blocks).reshape([-1 if axis == position else 1 for axis in range(len(shape))])
    return factor_of


def noise(key, extent, spread, most, cuts=(), kind=jnp.bfloat16):
    entries = spread * jax.random.normal(key, extent, jnp.float32)
    if cuts:
        entries = entries * block_levels(key, extent, cuts, -0.22, 0.18)
    return jnp.clip(entries, -most, most).astype(kind)


def setup_inputs(seed: int = 0) -> dict:
    keys = jax.random.split(jax.random.key(seed), 7)
    features = noise(keys[0], (NODES, FEAT), 1.0, 6.0, ((0, 32),))
    weight = noise(keys[1], (FEAT, FEAT), FEAT ** -0.5, 0.375)
    cotangent = noise(keys[2], (NODES, FEAT), 1.0, 6.0, ((0, 32),))
    block_rows = draw_block_rows(jax.random.fold_in(keys[6], 71), 0)
    block_counts = draw_block_counts(jax.random.fold_in(keys[6], 71), 0)
    block_values = draw_block_values(jax.random.fold_in(keys[6], 71), 0)
    return dict(features=features, weight=weight, cotangent=cotangent, block_rows=block_rows, block_counts=block_counts, block_values=block_values)


def adjacency_apply(node_rows, block_rows, block_counts, block_values):
    feats = node_rows.astype(jnp.float32).reshape(SLABS, SUBS, BLOCK, FEAT)
    slot_iota = jnp.arange(SLOTS).astype(jnp.int32)
    sub_iota = jnp.arange(SUBS).astype(jnp.int32)

    def one_row(row_index):
        rows_here = block_rows[row_index]
        counts_here = block_counts[row_index]
        values_here = block_values[row_index]

        def column_step(running, column_index):
            tile_now = values_here[column_index].astype(jnp.float32).reshape(SUBS, BLOCK, SLOTS, BLOCK)
            product = jnp.einsum('rakc,rcf->rkaf', tile_now, feats[column_index], precision=lax.Precision.HIGHEST)
            live_slots = (slot_iota[None, :] < counts_here[column_index][:, None]).astype(jnp.float32)
            selector = (rows_here[column_index][:, :, None] == sub_iota[None, None, :]).astype(jnp.float32)
            selector = selector * live_slots[:, :, None]
            running = running + jnp.einsum('rkn,rkaf->rnaf', selector, product, precision=lax.Precision.HIGHEST)
            return (running, None)
        running, _ = lax.scan(column_step, jnp.zeros((SUBS, SUBS, BLOCK, FEAT), jnp.float32), jnp.arange(SLABS).astype(jnp.int32))
        rounded = lax.optimization_barrier(running.astype(jnp.bfloat16)).astype(jnp.float32)
        return lax.optimization_barrier(jnp.sum(rounded, axis=0)).astype(jnp.bfloat16).reshape(SUBS * BLOCK, FEAT)
    return lax.map(one_row, jnp.arange(SLABS).astype(jnp.int32)).reshape(NODES, FEAT)

def reference(features, weight, cotangent, block_rows, block_counts, block_values):
    agg = adjacency_apply(features, block_rows, block_counts, block_values)
    pre = jnp.dot(agg, weight, preferred_element_type=jnp.float32)
    sig = jax.nn.sigmoid(pre)
    activation = (pre * sig).astype(jnp.bfloat16)
    dpre = (cotangent.astype(jnp.float32) * sig * (1.0 + pre * (1.0 - sig))).astype(jnp.bfloat16)
    grad_weight = jnp.dot(agg.T, dpre, preferred_element_type=jnp.float32) / math.sqrt(NODES)
    back = jnp.dot(dpre, weight.T, preferred_element_type=jnp.float32).astype(jnp.bfloat16)
    grad_features = adjacency_apply(back, block_rows, block_counts, block_values)
    return (activation, grad_weight, grad_features)
```

```python
import functools
import math

import jax
import jax.numpy as jnp
from jax import lax
from jax.experimental import pallas as pl
from jax.experimental.pallas import tpu as pltpu
from jax.sharding import PartitionSpec as P

F32 = jnp.float32
BF16 = jnp.bfloat16
VMEM_LIMIT = 8 * 1024 * 1024


def vmem():
    return pl.BlockSpec(memory_space=pltpu.VMEM)


def smem():
    return pl.BlockSpec(memory_space=pltpu.SMEM)


def params():
    return pltpu.CompilerParams(vmem_limit_bytes=VMEM_LIMIT)


def swap(value, axis, distance):
    size = lax.axis_size(axis)
    return lax.ppermute(value, axis, [(i, i ^ distance) for i in range(size)])


def dense_kernel(order, rows_ref, counts_ref, tiles_ref, out_ref):
    me, mine = lax.axis_index("blk"), lax.axis_index("rep")
    block = tiles_ref.shape[1]
    slots = tiles_ref.shape[2] // block
    subs = out_ref.shape[0] // block
    for q, distance in enumerate(order):
        slab = me ^ distance
        tile = tiles_ref[slab]
        places = [
            jnp.where(k < counts_ref[slab], rows_ref[slab, k] ^ mine, -1) for k in range(slots)
        ]
        for b in range(subs):
            value = jnp.zeros((block, block), tile.dtype)
            for k in range(slots):
                value = jnp.where(places[k] == b, tile[:, k * block : (k + 1) * block], value)
            out_ref[b * block : (b + 1) * block, q * block : (q + 1) * block] = value


def dense_adjacency(order, rows, counts, tiles):
    block = tiles.shape[1]
    shape = (lax.axis_size("rep") * block, len(order) * block)
    return pl.pallas_call(
        functools.partial(dense_kernel, order),
        out_shape=jax.ShapeDtypeStruct(shape, tiles.dtype),
        in_specs=[smem(), smem(), vmem()],
        out_specs=vmem(),
        compiler_params=params(),
        cost_estimate=pl.CostEstimate(flops=0, bytes_accessed=4 * tiles.size * 2, transcendentals=0),
    )(rows, counts, tiles)


def apply_kernel(n_pieces, dense_ref, *refs):
    pieces, outs = refs[:n_pieces], refs[n_pieces:]
    nodes = jnp.concatenate([piece[...] for piece in pieces], axis=0)
    block = outs[0].shape[0]
    for b in reversed(range(len(outs))):
        total = jnp.dot(
            dense_ref[b * block : (b + 1) * block, :], nodes, preferred_element_type=F32
        )
        outs[b][...] = total.astype(outs[b].dtype)


def apply_dense(dense, pieces):
    subs = lax.axis_size("rep")
    block, feat = dense.shape[0] // subs, pieces[0].shape[1]
    return pl.pallas_call(
        functools.partial(apply_kernel, len(pieces)),
        out_shape=[jax.ShapeDtypeStruct((block, feat), F32 if b == 0 else BF16) for b in range(subs)],
        in_specs=[vmem()] * (1 + len(pieces)),
        out_specs=[vmem()] * subs,
        compiler_params=params(),
        cost_estimate=pl.CostEstimate(
            flops=2 * dense.size * feat, bytes_accessed=2 * dense.size, transcendentals=0
        ),
    )(dense, *pieces)


def layer_kernel(n_parts, node_count, *refs):
    parts, (weight_ref, cotangent_ref, activation_ref, back_ref, grad_ref) = refs[:n_parts], refs[n_parts:]
    total = parts[0][...]
    for part in parts[1:]:
        total = total + part[...].astype(F32)
    agg = total.astype(BF16)
    weight = weight_ref[...]
    pre = jnp.dot(agg, weight, preferred_element_type=F32)
    sig = 1.0 / (1.0 + jnp.exp(-pre))
    activation_ref[...] = (pre * sig).astype(BF16)
    dpre = (cotangent_ref[...].astype(F32) * sig * (1.0 + pre * (1.0 - sig))).astype(BF16)
    back = lax.dot_general(dpre, weight, (((1,), (1,)), ((), ())), preferred_element_type=F32)
    back_ref[...] = back.astype(BF16)
    grad = lax.dot_general(agg, dpre, (((0,), (0,)), ((), ())), preferred_element_type=F32)
    grad_ref[...] = (grad * (1.0 / math.sqrt(node_count))).astype(grad_ref.dtype)


def layer(parts, weight, cotangent, node_count):
    block, feat = cotangent.shape
    small = jax.ShapeDtypeStruct((block, feat), BF16)
    return pl.pallas_call(
        functools.partial(layer_kernel, len(parts), node_count),
        out_shape=[small, small, jax.ShapeDtypeStruct((feat, feat), BF16)],
        in_specs=[vmem()] * (len(parts) + 2),
        out_specs=[vmem()] * 3,
        compiler_params=params(),
        cost_estimate=pl.CostEstimate(
            flops=6 * block * feat * feat, bytes_accessed=block * feat * 16, transcendentals=block * feat
        ),
    )(*parts, weight, cotangent)


def gather_direct(piece):
    size = lax.axis_size("blk")
    far = {d: swap(piece, "blk", d) for d in reversed(range(2, size, 2))}
    near = swap(piece, "blk", 1)
    mine = [far[d] for d in range(2, size, 2)]
    if not mine:
        return [piece, near]
    other = swap(jnp.concatenate(mine, axis=0), "blk", 1)
    return [piece, near] + mine + [other]


def gather_order(size):
    far = list(range(2, size, 2))
    return [0, 1] + far + [d + 1 for d in far]


def reduce_direct(parts):
    moved = {b: swap(parts[b], "rep", b) for b in reversed(range(1, len(parts)))}
    return [parts[0]] + [moved[b] for b in range(1, len(parts))]


def total_direct(value):
    for axis in ("blk", "rep"):
        distance = 1
        while distance < lax.axis_size(axis):
            value = lax.optimization_barrier(value)
            other = swap(value, axis, distance)
            value = value.astype(F32) + other.astype(F32)
            distance *= 2
            if not (axis == "rep" and distance >= lax.axis_size(axis)):
                value = value.astype(BF16)
    return value


def shards_direct(features, weight, cotangent, rows, counts, tiles):
    slabs = lax.axis_size("blk")
    node_count = features.shape[0] * slabs * lax.axis_size("rep")
    dense = dense_adjacency(gather_order(slabs), rows, counts, tiles)
    parts = reduce_direct(apply_dense(dense, gather_direct(features)))
    activation, back, grad = layer(parts, weight, cotangent, node_count)
    grad_weight = total_direct(grad)
    parts = reduce_direct(apply_dense(dense, gather_direct(back)))
    grad_features = parts[0]
    for part in parts[1:]:
        grad_features = grad_features + part.astype(F32)
    return activation, grad_weight.astype(F32), grad_features.astype(BF16)


def add_tile(running, column_block, node_slab, tiles, slot_rows, slot_counts):
    block_size = node_slab.shape[0]
    tile_now = lax.dynamic_index_in_dim(tiles, column_block, 0, keepdims=False)
    rows_now = lax.dynamic_index_in_dim(slot_rows, column_block, 0, keepdims=False)
    count_now = lax.dynamic_index_in_dim(slot_counts, column_block, 0, keepdims=False)

    def one_slot(slot_index, carried):
        weights_now = lax.dynamic_slice_in_dim(tile_now, slot_index * block_size, block_size, 1)
        product = jnp.dot(weights_now, node_slab, preferred_element_type=F32)
        first_row = rows_now[slot_index] * block_size
        current = lax.dynamic_slice_in_dim(carried, first_row, block_size, 0)
        return lax.dynamic_update_slice_in_dim(carried, current + product, first_row, 0)

    return lax.fori_loop(0, count_now, one_slot, running)


def aggregate(node_slab, tiles, slot_rows, slot_counts):
    block_size = node_slab.shape[0]
    running = jnp.zeros((block_size * lax.axis_size("rep"), node_slab.shape[1]), F32)
    piece = lax.all_gather(node_slab, "blk", axis=0, tiled=True)
    piece_count = piece.shape[0] // block_size

    def one_piece(inner, running_now):
        slab_now = lax.dynamic_slice_in_dim(piece, inner * block_size, block_size, 0)
        return add_tile(running_now, inner, slab_now, tiles, slot_rows, slot_counts)

    total = lax.fori_loop(0, piece_count, one_piece, running)
    return lax.psum_scatter(total.astype(BF16), "rep", scatter_dimension=0, tiled=True)


def shards_general(features, weight, cotangent, rows, counts, tiles):
    agg = aggregate(features, tiles, rows, counts)
    pre = jnp.dot(agg, weight, preferred_element_type=F32)
    sig = jax.nn.sigmoid(pre)
    activation = (pre * sig).astype(BF16)
    dpre = (cotangent.astype(F32) * sig * (1.0 + pre * (1.0 - sig))).astype(BF16)
    local_grad = lax.dot_general(agg, dpre, (((0,), (0,)), ((), ())), preferred_element_type=F32)
    node_count = features.shape[0] * lax.axis_size("blk") * lax.axis_size("rep")
    grad_weight = lax.psum(local_grad, ("blk", "rep")) / math.sqrt(node_count)
    back = lax.dot_general(dpre, weight, (((1,), (1,)), ((), ())), preferred_element_type=F32)
    return activation, grad_weight, aggregate(back.astype(BF16), tiles, rows, counts)


def shards(features, weight, cotangent, block_rows, block_counts, block_values):
    tiles = block_values[0, :, 0]
    rows = block_rows[0, :, 0]
    counts = block_counts[0, :, 0]
    sizes = lax.axis_size("blk"), lax.axis_size("rep")
    direct = all(size & (size - 1) == 0 for size in sizes) and sizes[0] <= 8 and sizes[1] <= 4
    return (shards_direct if direct else shards_general)(
        features, weight, cotangent, rows, counts, tiles
    )


def solution(mesh):
    placed = (
        P(("blk", "rep"), None),
        P(),
        P(("blk", "rep"), None),
        P("blk", None, "rep", None),
        P("blk", None, "rep"),
        P("blk", None, "rep", None, None),
    )
    return jax.shard_map(
        shards,
        mesh=mesh,
        in_specs=placed,
        out_specs=(P(("blk", "rep"), None), P(), P(("blk", "rep"), None)),
        check_vma=False,
    )
```

```python
import functools
import math

import jax
import jax.numpy as jnp
from jax import lax
from jax.experimental import pallas as pl
from jax.experimental.pallas import tpu as pltpu
from jax.sharding import PartitionSpec as P

F32 = jnp.float32
BF16 = jnp.bfloat16
VMEM_LIMIT = 8 * 1024 * 1024


def vmem():
    return pl.BlockSpec(memory_space=pltpu.VMEM)


def smem():
    return pl.BlockSpec(memory_space=pltpu.SMEM)


def params():
    return pltpu.CompilerParams(vmem_limit_bytes=VMEM_LIMIT)


def swap(value, axis, distance):
    size = lax.axis_size(axis)
    return lax.ppermute(value, axis, [(i, i ^ distance) for i in range(size)])


def far_order(slabs):
    return sorted(range(2, slabs, 2), key=lambda d: -bin(d).count("1"))


def sub_order(subs):
    return list(range(subs))[:0:-1]


def dense_kernel(order, subs, rows_ref, counts_ref, tiles_ref, out_ref):
    me, mine = lax.axis_index("blk"), lax.axis_index("rep")
    block = tiles_ref.shape[1]
    slots = tiles_ref.shape[2] // block
    for q, distance in enumerate(order):
        slab = me ^ distance
        tile = tiles_ref[slab]
        turned = [tile[:, k * block : (k + 1) * block].T for k in range(slots)]
        places = [
            jnp.where(k < counts_ref[slab], rows_ref[slab, k] ^ mine, -1) for k in range(slots)
        ]
        for b, sub in enumerate(subs):
            value = jnp.zeros((block, block), tile.dtype)
            for k in range(slots):
                value = jnp.where(places[k] == sub, turned[k], value)
            out_ref[q * block : (q + 1) * block, b * block : (b + 1) * block] = value


def dense_adjacency(order, subs, rows, counts, tiles):
    block = tiles.shape[1]
    shape = (len(order) * block, len(subs) * block)
    return pl.pallas_call(
        functools.partial(dense_kernel, order, subs),
        out_shape=jax.ShapeDtypeStruct(shape, tiles.dtype),
        in_specs=[smem(), smem(), vmem()],
        out_specs=vmem(),
        compiler_params=params(),
        cost_estimate=pl.CostEstimate(flops=0, bytes_accessed=4 * tiles.size * 2, transcendentals=0),
    )(rows, counts, tiles)


def apply_kernel(n_pieces, dense_ref, *refs):
    pieces, (odd_ref, even_ref) = refs[:n_pieces], refs[n_pieces:]
    nodes = jnp.concatenate([piece[...] for piece in pieces], axis=0)
    rows = odd_ref.shape[0]
    odd = jnp.dot(dense_ref[rows:, :], nodes, preferred_element_type=F32)
    odd_ref[...] = odd.astype(odd_ref.dtype)
    even_ref[...] = jnp.dot(dense_ref[:rows, :], nodes, preferred_element_type=F32)


def apply_dense(dense, pieces):
    shape = (dense.shape[0] // 2, pieces[0].shape[1])
    return pl.pallas_call(
        functools.partial(apply_kernel, len(pieces)),
        out_shape=[jax.ShapeDtypeStruct(shape, t) for t in (BF16, F32)],
        in_specs=[vmem()] * (1 + len(pieces)),
        out_specs=[vmem()] * 2,
        compiler_params=params(),
        cost_estimate=pl.CostEstimate(
            flops=2 * dense.size * shape[1], bytes_accessed=2 * dense.size, transcendentals=0
        ),
    )(dense, *pieces)


def chip_kernel(n_keep, even_ref, other_ref, *refs):
    keeps, (own_ref, *outs) = refs[:n_keep], refs[n_keep:]
    block, rows = own_ref.shape[0], even_ref.shape[0]
    own_ref[...] = even_ref[:block, :] + other_ref[:block, :].astype(F32)
    if keeps:
        half = (keeps[0][...] + other_ref[rows:, :].astype(F32)).astype(BF16)
        outs[-1][...] = half
        outs = outs[:-1]
    for q, out in enumerate(outs, 1):
        part = slice(q * block, (q + 1) * block)
        out[:block, :] = (even_ref[part, :] + other_ref[part, :].astype(F32)).astype(BF16)
        if keeps:
            out[block:, :] = half


def chip_sums(even, other, n_far, *keeps):
    block, feat = even.shape[0] // (1 + n_far), even.shape[1]
    more = keeps[0].shape[0] if keeps else 0
    shapes = [jax.ShapeDtypeStruct((block, feat), F32)]
    shapes += [jax.ShapeDtypeStruct((block + more, feat), BF16)] * n_far
    shapes += [jax.ShapeDtypeStruct((more, feat), BF16)] if keeps else []
    return pl.pallas_call(
        functools.partial(chip_kernel, len(keeps)),
        out_shape=shapes,
        in_specs=[vmem()] * (2 + len(keeps)),
        out_specs=[vmem()] * len(shapes),
        compiler_params=params(),
        cost_estimate=pl.CostEstimate(flops=4 * even.size, bytes_accessed=4 * even.size, transcendentals=0),
    )(even, other, *keeps)


def tree(order, values):
    values = [value.astype(F32) for _, value in sorted(zip(order, values), key=lambda pair: pair[0])]
    while len(values) > 1:
        values = [values[k] + values[k + 1] for k in range(0, len(values), 2)]
    return values[0]


def layer_kernel(n_parts, *refs):
    parts, (weight_ref, cotangent_ref, pair_ref) = refs[:n_parts], refs[n_parts:]
    block = cotangent_ref.shape[0]
    total = parts[0][...]
    for part in parts[1:]:
        total = total + part[...].astype(F32)
    agg = total.astype(BF16)
    pre = jnp.dot(agg, weight_ref[...], preferred_element_type=F32)
    sig = 1.0 / (1.0 + jnp.exp(-pre))
    dpre = cotangent_ref[...].astype(F32) * sig * (1.0 + pre * (1.0 - sig))
    pair_ref[:block, :] = agg
    pair_ref[block:, :] = dpre.astype(BF16)


def layer(parts, weight, cotangent):
    block, feat = cotangent.shape
    return pl.pallas_call(
        functools.partial(layer_kernel, len(parts)),
        out_shape=jax.ShapeDtypeStruct((2 * block, feat), BF16),
        in_specs=[vmem()] * (len(parts) + 2),
        out_specs=vmem(),
        compiler_params=params(),
        cost_estimate=pl.CostEstimate(
            flops=2 * block * feat * feat, bytes_accessed=block * feat * 16, transcendentals=block * feat
        ),
    )(*parts, weight, cotangent)


def activation_kernel(pair_ref, weight_ref, out_ref):
    pre = jnp.dot(pair_ref[: out_ref.shape[0], :], weight_ref[...], preferred_element_type=F32)
    out_ref[...] = (pre / (1.0 + jnp.exp(-pre))).astype(out_ref.dtype)


def layer_output(pair, weight):
    shape = (pair.shape[0] // 2, pair.shape[1])
    return pl.pallas_call(
        activation_kernel,
        out_shape=jax.ShapeDtypeStruct(shape, BF16),
        in_specs=[vmem()] * 2,
        out_specs=vmem(),
        compiler_params=params(),
        cost_estimate=pl.CostEstimate(
            flops=pair.size * shape[1], bytes_accessed=pair.size * 4, transcendentals=pair.size // 2
        ),
    )(pair, weight)


def back_kernel(scale, n_pairs, dense_ref, weight_ref, *refs):
    pairs, (odd_ref, even_ref, keep_ref) = refs[:n_pairs], refs[n_pairs:]
    block = pairs[0].shape[0] // 2
    dpre = jnp.concatenate([pair[block:, :] for pair in pairs], axis=0)
    back = lax.dot_general(
        dpre, weight_ref[...], (((1,), (1,)), ((), ())), preferred_element_type=F32
    ).astype(BF16)
    rows = even_ref.shape[0]
    odd = jnp.dot(dense_ref[rows:, :], back, preferred_element_type=F32)
    odd_ref[:rows, :] = odd.astype(odd_ref.dtype)
    even_ref[...] = jnp.dot(dense_ref[:rows, :], back, preferred_element_type=F32)
    agg = jnp.concatenate([pair[:block, :] for pair in pairs], axis=0)
    half = agg.shape[1] // 2
    first, second = (
        lax.dot_general(cols, dpre, (((0,), (0,)), ((), ())), preferred_element_type=F32) * scale
        for cols in (agg[:, :half], agg[:, half:])
    )
    is_first = lax.axis_index("blk") % 2 == 0
    odd_ref[rows:, :] = jnp.where(is_first, second, first).astype(odd_ref.dtype)
    keep_ref[...] = jnp.where(is_first, first, second)


def apply_back(dense, weight, pairs, scale):
    rows, feat = dense.shape[0] // 2, weight.shape[0]
    half = feat // 2
    shapes = ((rows + half, BF16), (rows, F32), (half, F32))
    return pl.pallas_call(
        functools.partial(back_kernel, scale, len(pairs)),
        out_shape=[jax.ShapeDtypeStruct((n, feat), t) for n, t in shapes],
        in_specs=[vmem()] * (2 + len(pairs)),
        out_specs=[vmem()] * 3,
        compiler_params=params(),
        cost_estimate=pl.CostEstimate(
            flops=4 * dense.size * feat, bytes_accessed=2 * dense.size, transcendentals=0
        ),
    )(dense, weight, *pairs)


def half_kernel(order, half_ref, *refs):
    parts, out_ref = refs[:-1], refs[-1]
    more = half_ref.shape[0]
    out_ref[...] = tree(order, [half_ref[...]] + [part[-more:, :] for part in parts])


def half_sum(order, half, parts):
    return pl.pallas_call(
        functools.partial(half_kernel, order),
        out_shape=jax.ShapeDtypeStruct(half.shape, F32),
        in_specs=[vmem()] * (1 + len(parts)),
        out_specs=vmem(),
        compiler_params=params(),
        cost_estimate=pl.CostEstimate(flops=half.size * 4, bytes_accessed=half.size * 12, transcendentals=0),
    )(half, *parts)


def last_kernel(own_ref, *refs):
    parts, out_ref = refs[:-1], refs[-1]
    total = own_ref[...]
    for part in parts:
        total = total + part[: own_ref.shape[0], :].astype(F32)
    out_ref[...] = total.astype(out_ref.dtype)


def last_sum(own, parts):
    return pl.pallas_call(
        last_kernel,
        out_shape=jax.ShapeDtypeStruct(own.shape, BF16),
        in_specs=[vmem()] * (1 + len(parts)),
        out_specs=vmem(),
        compiler_params=params(),
        cost_estimate=pl.CostEstimate(flops=own.size * 4, bytes_accessed=own.size * 12, transcendentals=0),
    )(own, *parts)


def exchange(value, axis, distances):
    return [value] + [swap(value, axis, d) for d in distances]


def join(mine):
    other = swap(mine, "blk", 1)
    is_first = lax.axis_index("blk") % 2 == 0
    return jnp.where(
        is_first, jnp.concatenate([mine, other], axis=0), jnp.concatenate([other, mine], axis=0)
    )


def shards_direct(features, weight, cotangent, rows, counts, tiles):
    slabs, subs = lax.axis_size("blk"), lax.axis_size("rep")
    far, near = far_order(slabs), sub_order(subs)
    node_count = features.shape[0] * slabs * subs
    even = [0] + far
    dense = dense_adjacency(even + [d + 1 for d in even], [0] + near, rows, counts, tiles)
    pieces, dense = lax.optimization_barrier((exchange(features, "rep", near), dense))
    odd, mine = apply_dense(dense, pieces)
    own, *sums = chip_sums(mine, swap(odd, "blk", 1), len(far))
    parts = [swap(value, "blk", d) for value, d in zip(sums, far)]
    pair = layer([own] + parts, weight, cotangent)
    pairs = exchange(pair, "rep", near)
    activation = layer_output(pair, weight)
    pairs, activation = lax.optimization_barrier((pairs, activation))
    odd, mine, keep = apply_back(dense, weight, pairs, 1.0 / math.sqrt(node_count))
    own, *sums, half = chip_sums(mine, swap(odd, "blk", 1), len(far), keep)
    parts = [swap(value, "blk", d) for value, d in zip(sums, far)]
    grad = join(half_sum(even, half, parts))
    return activation, grad, last_sum(own, parts)


def add_tile(running, column_block, node_slab, tiles, slot_rows, slot_counts):
    block_size = node_slab.shape[0]
    tile_now = lax.dynamic_index_in_dim(tiles, column_block, 0, keepdims=False)
    rows_now = lax.dynamic_index_in_dim(slot_rows, column_block, 0, keepdims=False)
    count_now = lax.dynamic_index_in_dim(slot_counts, column_block, 0, keepdims=False)

    def one_slot(slot_index, carried):
        weights_now = lax.dynamic_slice_in_dim(tile_now, slot_index * block_size, block_size, 1)
        product = jnp.dot(weights_now, node_slab, preferred_element_type=F32)
        first_row = rows_now[slot_index] * block_size
        current = lax.dynamic_slice_in_dim(carried, first_row, block_size, 0)
        return lax.dynamic_update_slice_in_dim(carried, current + product, first_row, 0)

    return lax.fori_loop(0, count_now, one_slot, running)


def aggregate(node_slab, tiles, slot_rows, slot_counts):
    block_size = node_slab.shape[0]
    running = jnp.zeros((block_size * lax.axis_size("rep"), node_slab.shape[1]), F32)
    piece = lax.all_gather(node_slab, "blk", axis=0, tiled=True)
    piece_count = piece.shape[0] // block_size

    def one_piece(inner, running_now):
        slab_now = lax.dynamic_slice_in_dim(piece, inner * block_size, block_size, 0)
        return add_tile(running_now, inner, slab_now, tiles, slot_rows, slot_counts)

    total = lax.fori_loop(0, piece_count, one_piece, running)
    return lax.psum_scatter(total.astype(BF16), "rep", scatter_dimension=0, tiled=True)


def shards_general(features, weight, cotangent, rows, counts, tiles):
    agg = aggregate(features, tiles, rows, counts)
    pre = jnp.dot(agg, weight, preferred_element_type=F32)
    sig = jax.nn.sigmoid(pre)
    activation = (pre * sig).astype(BF16)
    dpre = (cotangent.astype(F32) * sig * (1.0 + pre * (1.0 - sig))).astype(BF16)
    local_grad = lax.dot_general(agg, dpre, (((0,), (0,)), ((), ())), preferred_element_type=F32)
    node_count = features.shape[0] * lax.axis_size("blk") * lax.axis_size("rep")
    grad_weight = lax.psum(local_grad, ("blk", "rep")) / math.sqrt(node_count)
    back = lax.dot_general(dpre, weight, (((1,), (1,)), ((), ())), preferred_element_type=F32)
    return activation, grad_weight, aggregate(back.astype(BF16), tiles, rows, counts)


def shards(features, weight, cotangent, block_rows, block_counts, block_values):
    tiles = block_values[0, :, 0]
    rows = block_rows[0, :, 0]
    counts = block_counts[0, :, 0]
    sizes = lax.axis_size("blk"), lax.axis_size("rep")
    direct = sizes[0] in (4, 8) and sizes[1] in (2, 4)
    return (shards_direct if direct else shards_general)(
        features, weight, cotangent, rows, counts, tiles
    )


def solution(mesh):
    placed = (
        P(("blk", "rep"), None),
        P(),
        P(("blk", "rep"), None),
        P("blk", None, "rep", None),
        P("blk", None, "rep"),
        P("blk", None, "rep", None, None),
    )
    return jax.shard_map(
        shards,
        mesh=mesh,
        in_specs=placed,
        out_specs=(P(("blk", "rep"), None), P(), P(("blk", "rep"), None)),
        check_vma=False,
    )
```

```python
import functools
import math

import jax
import jax.numpy as jnp
from jax import lax
from jax.experimental import pallas as pl
from jax.experimental.pallas import tpu as pltpu
from jax.sharding import PartitionSpec as P

F32 = jnp.float32
BF16 = jnp.bfloat16
VMEM_LIMIT = 8 * 1024 * 1024


def vmem():
    return pl.BlockSpec(memory_space=pltpu.VMEM)


def smem():
    return pl.BlockSpec(memory_space=pltpu.SMEM)


def params():
    return pltpu.CompilerParams(vmem_limit_bytes=VMEM_LIMIT)


def swap(value, axis, distance):
    size = lax.axis_size(axis)
    return lax.ppermute(value, axis, [(i, i ^ distance) for i in range(size)])


def far_order(slabs):
    return sorted(range(2, slabs, 2), key=lambda d: -bin(d).count("1"))


def sub_order(subs):
    return [2, 3, 1] if subs == 4 else [1]


def dense_kernel(order, subs, rows_ref, counts_ref, tiles_ref, out_ref):
    me, mine = lax.axis_index("blk"), lax.axis_index("rep")
    block = tiles_ref.shape[1]
    slots = tiles_ref.shape[2] // block
    for q, distance in enumerate(order):
        slab = me ^ distance
        tile = tiles_ref[slab]
        turned = [tile[:, k * block : (k + 1) * block].T for k in range(slots)]
        places = [
            jnp.where(k < counts_ref[slab], rows_ref[slab, k] ^ mine, -1) for k in range(slots)
        ]
        for b, sub in enumerate(subs):
            value = jnp.zeros((block, block), tile.dtype)
            for k in range(slots):
                value = jnp.where(places[k] == sub, turned[k], value)
            out_ref[q * block : (q + 1) * block, b * block : (b + 1) * block] = value


def dense_adjacency(order, subs, rows, counts, tiles):
    block = tiles.shape[1]
    shape = (len(order) * block, len(subs) * block)
    return pl.pallas_call(
        functools.partial(dense_kernel, order, subs),
        out_shape=jax.ShapeDtypeStruct(shape, tiles.dtype),
        in_specs=[smem(), smem(), vmem()],
        out_specs=vmem(),
        compiler_params=params(),
        cost_estimate=pl.CostEstimate(flops=0, bytes_accessed=4 * tiles.size * 2, transcendentals=0),
    )(rows, counts, tiles)


def first_kernel(n_pieces, dense_ref, *refs):
    nodes = jnp.concatenate([piece[...] for piece in refs[:n_pieces]], axis=0)
    out_ref = refs[-1]
    half = dense_ref.shape[0] // 2
    rows = dense_ref[half : half + out_ref.shape[0], :]
    out_ref[...] = jnp.dot(rows, nodes, preferred_element_type=F32).astype(out_ref.dtype)


def apply_first(dense, pieces):
    shape = pieces[0].shape
    return pl.pallas_call(
        functools.partial(first_kernel, len(pieces)),
        out_shape=jax.ShapeDtypeStruct(shape, BF16),
        in_specs=[vmem()] * (1 + len(pieces)),
        out_specs=vmem(),
        compiler_params=params(),
        cost_estimate=pl.CostEstimate(
            flops=2 * dense.shape[1] * shape[0] * shape[1], bytes_accessed=dense.size // 4, transcendentals=0
        ),
    )(dense, *pieces)


def rest_kernel(n_pieces, dense_ref, *refs):
    nodes = jnp.concatenate([piece[...] for piece in refs[:n_pieces]], axis=0)
    odd_ref, even_ref = refs[n_pieces:]
    half = dense_ref.shape[0] // 2
    rows = dense_ref[dense_ref.shape[0] - odd_ref.shape[0] :, :]
    odd_ref[...] = jnp.dot(rows, nodes, preferred_element_type=F32).astype(odd_ref.dtype)
    even_ref[...] = jnp.dot(dense_ref[:half, :], nodes, preferred_element_type=F32)


def apply_rest(dense, pieces, block):
    rows, feat = dense.shape[0] // 2, pieces[0].shape[1]
    return pl.pallas_call(
        functools.partial(rest_kernel, len(pieces)),
        out_shape=[jax.ShapeDtypeStruct((rows - block, feat), BF16), jax.ShapeDtypeStruct((rows, feat), F32)],
        in_specs=[vmem()] * (1 + len(pieces)),
        out_specs=[vmem()] * 2,
        compiler_params=params(),
        cost_estimate=pl.CostEstimate(
            flops=2 * dense.size * feat, bytes_accessed=2 * dense.size, transcendentals=0
        ),
    )(dense, *pieces)


def first_sum_kernel(even_ref, other_ref, *refs):
    block = even_ref.shape[0]
    if len(refs) == 1:
        refs[0][...] = (even_ref[...] + other_ref[...].astype(F32)).astype(BF16)
        return
    keep_ref, out_ref, half_ref = refs
    out_ref[:block, :] = (even_ref[...] + other_ref[:block, :].astype(F32)).astype(BF16)
    half = (keep_ref[...] + other_ref[block:, :].astype(F32)).astype(BF16)
    out_ref[block:, :] = half
    half_ref[...] = half


def first_sum(even, other, block, *keep):
    shapes = [jax.ShapeDtypeStruct(other.shape, BF16)]
    shapes += [jax.ShapeDtypeStruct(half.shape, BF16) for half in keep]
    top = pl.BlockSpec((block, even.shape[1]), lambda i: (0, 0))
    return pl.pallas_call(
        first_sum_kernel,
        grid=(1,),
        out_shape=shapes,
        in_specs=[top] + [vmem()] * (1 + len(keep)),
        out_specs=[vmem()] * len(shapes),
        compiler_params=params(),
        cost_estimate=pl.CostEstimate(flops=other.size, bytes_accessed=other.size * 8, transcendentals=0),
    )(even, other, *keep)


def rest_sum_kernel(n_half, even_ref, other_ref, *refs):
    half, (own_ref, *outs) = refs[:n_half], refs[n_half:]
    block = own_ref.shape[0]
    for q, out in enumerate([own_ref] + outs):
        total = even_ref[(q + 1) * block : (q + 2) * block, :]
        total = total + other_ref[q * block : (q + 1) * block, :].astype(F32)
        out[:block, :] = total.astype(out.dtype)
        if half and q:
            out[block:, :] = half[0][...]


def rest_sums(even, other, block, *half):
    feat = even.shape[1]
    more = half[0].shape[0] if half else 0
    n_out = other.shape[0] // block - 1
    shapes = [jax.ShapeDtypeStruct((block, feat), F32)]
    shapes += [jax.ShapeDtypeStruct((block + more, feat), BF16)] * n_out
    return pl.pallas_call(
        functools.partial(rest_sum_kernel, len(half)),
        out_shape=shapes,
        in_specs=[vmem()] * (2 + len(half)),
        out_specs=[vmem()] * len(shapes),
        compiler_params=params(),
        cost_estimate=pl.CostEstimate(flops=other.size, bytes_accessed=other.size * 8, transcendentals=0),
    )(even, other, *half)


def tree(order, values):
    values = [value.astype(F32) for _, value in sorted(zip(order, values), key=lambda pair: pair[0])]
    while len(values) > 1:
        values = [values[k] + values[k + 1] for k in range(0, len(values), 2)]
    return values[0]


def layer_kernel(n_parts, *refs):
    parts, (weight_ref, cotangent_ref, pair_ref) = refs[:n_parts], refs[n_parts:]
    block = cotangent_ref.shape[0]
    total = parts[0][...]
    for part in parts[1:]:
        total = total + part[...].astype(F32)
    agg = total.astype(BF16)
    pre = jnp.dot(agg, weight_ref[...], preferred_element_type=F32)
    sig = 1.0 / (1.0 + jnp.exp(-pre))
    dpre = cotangent_ref[...].astype(F32) * sig * (1.0 + pre * (1.0 - sig))
    pair_ref[:block, :] = agg
    pair_ref[block:, :] = dpre.astype(BF16)


def layer(parts, weight, cotangent):
    block, feat = cotangent.shape
    return pl.pallas_call(
        functools.partial(layer_kernel, len(parts)),
        out_shape=jax.ShapeDtypeStruct((2 * block, feat), BF16),
        in_specs=[vmem()] * (len(parts) + 2),
        out_specs=vmem(),
        compiler_params=params(),
        cost_estimate=pl.CostEstimate(
            flops=2 * block * feat * feat, bytes_accessed=block * feat * 16, transcendentals=block * feat
        ),
    )(*parts, weight, cotangent)


def activation_kernel(pair_ref, weight_ref, out_ref):
    pre = jnp.dot(pair_ref[: out_ref.shape[0], :], weight_ref[...], preferred_element_type=F32)
    out_ref[...] = (pre / (1.0 + jnp.exp(-pre))).astype(out_ref.dtype)


def layer_output(pair, weight):
    shape = (pair.shape[0] // 2, pair.shape[1])
    return pl.pallas_call(
        activation_kernel,
        out_shape=jax.ShapeDtypeStruct(shape, BF16),
        in_specs=[vmem()] * 2,
        out_specs=vmem(),
        compiler_params=params(),
        cost_estimate=pl.CostEstimate(
            flops=pair.size * shape[1], bytes_accessed=pair.size * 4, transcendentals=pair.size // 2
        ),
    )(pair, weight)


def back_kernel(scale, n_pairs, dense_ref, weight_ref, *refs):
    pairs, (back_ref, first_ref, keep_ref) = refs[:n_pairs], refs[n_pairs:]
    block = pairs[0].shape[0] // 2
    dpre = jnp.concatenate([pair[block:, :] for pair in pairs], axis=0)
    back = lax.dot_general(
        dpre, weight_ref[...], (((1,), (1,)), ((), ())), preferred_element_type=F32
    ).astype(BF16)
    back_ref[...] = back
    rows = dense_ref.shape[0] // 2
    first = jnp.dot(dense_ref[rows : rows + block, :], back, preferred_element_type=F32)
    first_ref[:block, :] = first.astype(BF16)
    agg = jnp.concatenate([pair[:block, :] for pair in pairs], axis=0)
    half = agg.shape[1] // 2
    upper, lower = (
        lax.dot_general(cols, dpre, (((0,), (0,)), ((), ())), preferred_element_type=F32) * scale
        for cols in (agg[:, :half], agg[:, half:])
    )
    is_first = lax.axis_index("blk") % 2 == 0
    first_ref[block:, :] = jnp.where(is_first, lower, upper).astype(BF16)
    keep_ref[...] = jnp.where(is_first, upper, lower)


def apply_back(dense, weight, pairs, scale):
    feat = weight.shape[0]
    block, half = pairs[0].shape[0] // 2, feat // 2
    shapes = ((len(pairs) * block, BF16), (block + half, BF16), (half, F32))
    return pl.pallas_call(
        functools.partial(back_kernel, scale, len(pairs)),
        out_shape=[jax.ShapeDtypeStruct((n, feat), t) for n, t in shapes],
        in_specs=[vmem()] * (2 + len(pairs)),
        out_specs=[vmem()] * 3,
        compiler_params=params(),
        cost_estimate=pl.CostEstimate(
            flops=8 * len(pairs) * block * feat * feat, bytes_accessed=dense.size, transcendentals=0
        ),
    )(dense, weight, *pairs)


def half_kernel(order, half_ref, *refs):
    parts, out_ref = refs[:-1], refs[-1]
    more = half_ref.shape[0]
    total = tree(order, [half_ref[...]] + [part[-more:, :] for part in parts])
    out_ref[...] = total.astype(out_ref.dtype)


def half_sum(order, half, parts):
    return pl.pallas_call(
        functools.partial(half_kernel, order),
        out_shape=jax.ShapeDtypeStruct(half.shape, BF16),
        in_specs=[vmem()] * (1 + len(parts)),
        out_specs=vmem(),
        compiler_params=params(),
        cost_estimate=pl.CostEstimate(flops=half.size * 4, bytes_accessed=half.size * 12, transcendentals=0),
    )(half, *parts)


def last_kernel(own_ref, *refs):
    parts, out_ref = refs[:-1], refs[-1]
    total = own_ref[...]
    for part in parts:
        total = total + part[: own_ref.shape[0], :].astype(F32)
    out_ref[...] = total.astype(out_ref.dtype)


def last_sum(own, parts):
    return pl.pallas_call(
        last_kernel,
        out_shape=jax.ShapeDtypeStruct(own.shape, BF16),
        in_specs=[vmem()] * (1 + len(parts)),
        out_specs=vmem(),
        compiler_params=params(),
        cost_estimate=pl.CostEstimate(flops=own.size * 4, bytes_accessed=own.size * 12, transcendentals=0),
    )(own, *parts)


def exchange(value, axis, distances):
    return [value] + [swap(value, axis, d) for d in distances]


def join(mine):
    other = swap(mine, "blk", 1)
    is_first = lax.axis_index("blk") % 2 == 0
    return jnp.where(
        is_first, jnp.concatenate([mine, other], axis=0), jnp.concatenate([other, mine], axis=0)
    )


def shards_direct(features, weight, cotangent, rows, counts, tiles):
    block = features.shape[0]
    slabs, subs = lax.axis_size("blk"), lax.axis_size("rep")
    far, near = far_order(slabs), sub_order(subs)
    node_count = block * slabs * subs
    even = far[:1] + [0] + far[1:]
    dense = dense_adjacency(even + [d + 1 for d in even], [0] + near, rows, counts, tiles)

    pieces, dense = lax.optimization_barrier((exchange(features, "rep", near), dense))
    other = swap(apply_first(dense, pieces), "blk", 1)
    rest, mine = apply_rest(dense, pieces, block)
    rest, other = lax.optimization_barrier((rest, other))
    (first,) = first_sum(mine, other, block)
    own, *sums = rest_sums(mine, swap(rest, "blk", 1), block)
    parts = [swap(value, "blk", d) for value, d in zip([first] + sums, far)]

    pair = layer([own] + parts, weight, cotangent)
    pairs = exchange(pair, "rep", near)
    activation = layer_output(pair, weight)
    pairs, activation = lax.optimization_barrier((pairs, activation))
    back, first, keep = apply_back(dense, weight, pairs, 1.0 / math.sqrt(node_count))
    other = swap(first, "blk", 1)
    rest, mine = apply_rest(dense, [back], block)
    rest, other = lax.optimization_barrier((rest, other))
    first, half = first_sum(mine, other, block, keep)
    own, *sums = rest_sums(mine, swap(rest, "blk", 1), block, half)
    parts = [swap(value, "blk", d) for value, d in zip([first] + sums, far)]
    grad = join(half_sum([0] + far, half, parts)).astype(F32)
    return activation, grad, last_sum(own, parts)


def add_tile(running, column_block, node_slab, tiles, slot_rows, slot_counts):
    block_size = node_slab.shape[0]
    tile_now = lax.dynamic_index_in_dim(tiles, column_block, 0, keepdims=False)
    rows_now = lax.dynamic_index_in_dim(slot_rows, column_block, 0, keepdims=False)
    count_now = lax.dynamic_index_in_dim(slot_counts, column_block, 0, keepdims=False)

    def one_slot(slot_index, carried):
        weights_now = lax.dynamic_slice_in_dim(tile_now, slot_index * block_size, block_size, 1)
        product = jnp.dot(weights_now, node_slab, preferred_element_type=F32)
        first_row = rows_now[slot_index] * block_size
        current = lax.dynamic_slice_in_dim(carried, first_row, block_size, 0)
        return lax.dynamic_update_slice_in_dim(carried, current + product, first_row, 0)

    return lax.fori_loop(0, count_now, one_slot, running)


def aggregate(node_slab, tiles, slot_rows, slot_counts):
    block_size = node_slab.shape[0]
    running = jnp.zeros((block_size * lax.axis_size("rep"), node_slab.shape[1]), F32)
    piece = lax.all_gather(node_slab, "blk", axis=0, tiled=True)
    piece_count = piece.shape[0] // block_size

    def one_piece(inner, running_now):
        slab_now = lax.dynamic_slice_in_dim(piece, inner * block_size, block_size, 0)
        return add_tile(running_now, inner, slab_now, tiles, slot_rows, slot_counts)

    total = lax.fori_loop(0, piece_count, one_piece, running)
    return lax.psum_scatter(total.astype(BF16), "rep", scatter_dimension=0, tiled=True)


def shards_general(features, weight, cotangent, rows, counts, tiles):
    agg = aggregate(features, tiles, rows, counts)
    pre = jnp.dot(agg, weight, preferred_element_type=F32)
    sig = jax.nn.sigmoid(pre)
    activation = (pre * sig).astype(BF16)
    dpre = (cotangent.astype(F32) * sig * (1.0 + pre * (1.0 - sig))).astype(BF16)
    local_grad = lax.dot_general(agg, dpre, (((0,), (0,)), ((), ())), preferred_element_type=F32)
    node_count = features.shape[0] * lax.axis_size("blk") * lax.axis_size("rep")
    grad_weight = lax.psum(local_grad, ("blk", "rep")) / math.sqrt(node_count)
    back = lax.dot_general(dpre, weight, (((1,), (1,)), ((), ())), preferred_element_type=F32)
    return activation, grad_weight, aggregate(back.astype(BF16), tiles, rows, counts)


def shards(features, weight, cotangent, block_rows, block_counts, block_values):
    tiles = block_values[0, :, 0]
    rows = block_rows[0, :, 0]
    counts = block_counts[0, :, 0]
    sizes = lax.axis_size("blk"), lax.axis_size("rep")
    direct = sizes[0] in (4, 8) and sizes[1] in (2, 4)
    return (shards_direct if direct else shards_general)(
        features, weight, cotangent, rows, counts, tiles
    )


def solution(mesh):
    placed = (
        P(("blk", "rep"), None),
        P(),
        P(("blk", "rep"), None),
        P("blk", None, "rep", None),
        P("blk", None, "rep"),
        P("blk", None, "rep", None, None),
    )
    return jax.shard_map(
        shards,
        mesh=mesh,
        in_specs=placed,
        out_specs=(P(("blk", "rep"), None), P(), P(("blk", "rep"), None)),
        check_vma=False,
    )
```

```python
import functools
import math

import jax
import jax.numpy as jnp
from jax import lax
from jax.experimental import pallas as pl
from jax.experimental.pallas import tpu as pltpu
from jax.sharding import PartitionSpec as P

F32 = jnp.float32
BF16 = jnp.bfloat16
ROWS = (((0,), (0,)), ((), ()))
VMEM_LIMIT = 8 * 1024 * 1024


def vmem():
    return pl.BlockSpec(memory_space=pltpu.VMEM)


def smem():
    return pl.BlockSpec(memory_space=pltpu.SMEM)


def params():
    return pltpu.CompilerParams(vmem_limit_bytes=VMEM_LIMIT)


def send(value, axis, step):
    return lax.ppermute(value, axis, [(i, step(i)) for i in range(lax.axis_size(axis))])


def at(distance):
    return lambda i: i ^ distance


def far_steps(slabs):
    if slabs == 8:
        return [at(6), at(2), at(4)]
    return [at(2)]


def sub_order(subs):
    return [2, 3, 1] if subs == 4 else [1]


def dense_kernel(steps, subs, rows_ref, counts_ref, tiles_ref, out_ref):
    me, mine = lax.axis_index("blk"), lax.axis_index("rep")
    block = tiles_ref.shape[1]
    slots = tiles_ref.shape[2] // block
    for q, step in enumerate(steps):
        slab = step(me)
        tile = tiles_ref[slab]
        turned = [tile[:, k * block : (k + 1) * block].T for k in range(slots)]
        places = [
            jnp.where(k < counts_ref[slab], rows_ref[slab, k] ^ mine, -1) for k in range(slots)
        ]
        for b, sub in enumerate(subs):
            value = jnp.zeros((block, block), tile.dtype)
            for k in range(slots):
                value = jnp.where(places[k] == sub, turned[k], value)
            out_ref[q * block : (q + 1) * block, b * block : (b + 1) * block] = value


def dense_adjacency(steps, subs, rows, counts, tiles):
    block = tiles.shape[1]
    shape = (len(steps) * block, len(subs) * block)
    return pl.pallas_call(
        functools.partial(dense_kernel, steps, subs),
        out_shape=jax.ShapeDtypeStruct(shape, tiles.dtype),
        in_specs=[smem(), smem(), vmem()],
        out_specs=vmem(),
        compiler_params=params(),
        cost_estimate=pl.CostEstimate(flops=0, bytes_accessed=4 * tiles.size * 2, transcendentals=0),
    )(rows, counts, tiles)


def first_kernel(n_pieces, dense_ref, *refs):
    nodes = jnp.concatenate([piece[...] for piece in refs[:n_pieces]], axis=0)
    out_ref = refs[-1]
    half = dense_ref.shape[0] // 2
    rows = dense_ref[half : half + out_ref.shape[0], :]
    out_ref[...] = jnp.dot(rows, nodes, preferred_element_type=F32).astype(out_ref.dtype)


def apply_first(dense, pieces):
    shape = pieces[0].shape
    return pl.pallas_call(
        functools.partial(first_kernel, len(pieces)),
        out_shape=jax.ShapeDtypeStruct(shape, BF16),
        in_specs=[vmem()] * (1 + len(pieces)),
        out_specs=vmem(),
        compiler_params=params(),
        cost_estimate=pl.CostEstimate(
            flops=2 * dense.shape[1] * shape[0] * shape[1], bytes_accessed=dense.size // 4, transcendentals=0
        ),
    )(dense, *pieces)


def rest_kernel(block, n_pieces, dense_ref, *refs):
    nodes = jnp.concatenate([piece[-block:, :] for piece in refs[:n_pieces]], axis=0)
    odd_ref, even_ref = refs[n_pieces:]
    half = dense_ref.shape[0] // 2
    rows = dense_ref[dense_ref.shape[0] - odd_ref.shape[0] :, :]
    odd_ref[...] = jnp.dot(rows, nodes, preferred_element_type=F32).astype(odd_ref.dtype)
    even_ref[...] = jnp.dot(dense_ref[:half, :], nodes, preferred_element_type=F32)


def apply_rest(dense, pieces, block):
    rows, feat = dense.shape[0] // 2, pieces[0].shape[1]
    return pl.pallas_call(
        functools.partial(rest_kernel, block, len(pieces)),
        out_shape=[jax.ShapeDtypeStruct((rows - block, feat), BF16), jax.ShapeDtypeStruct((rows, feat), F32)],
        in_specs=[vmem()] * (1 + len(pieces)),
        out_specs=[vmem()] * 2,
        compiler_params=params(),
        cost_estimate=pl.CostEstimate(
            flops=2 * dense.size * feat, bytes_accessed=2 * dense.size, transcendentals=0
        ),
    )(dense, *pieces)


def first_sum_kernel(even_ref, other_ref, *refs):
    block = even_ref.shape[0]
    if len(refs) == 1:
        refs[0][...] = (even_ref[...] + other_ref[...].astype(F32)).astype(BF16)
        return
    keep_ref, out_ref, half_ref = refs
    out_ref[:block, :] = (even_ref[...] + other_ref[:block, :].astype(F32)).astype(BF16)
    half = (keep_ref[...] + other_ref[block:, :].astype(F32)).astype(BF16)
    out_ref[block:, :] = half
    half_ref[...] = half


def first_sum(even, other, block, *keep):
    shapes = [jax.ShapeDtypeStruct(other.shape, BF16)]
    shapes += [jax.ShapeDtypeStruct(half.shape, BF16) for half in keep]
    top = pl.BlockSpec((block, even.shape[1]), lambda i: (0, 0))
    return pl.pallas_call(
        first_sum_kernel,
        grid=(1,),
        out_shape=shapes,
        in_specs=[top] + [vmem()] * (1 + len(keep)),
        out_specs=[vmem()] * len(shapes),
        compiler_params=params(),
        cost_estimate=pl.CostEstimate(flops=other.size, bytes_accessed=other.size * 8, transcendentals=0),
    )(even, other, *keep)


def rest_sum_kernel(n_half, even_ref, other_ref, *refs):
    half, (own_ref, *outs) = refs[:n_half], refs[n_half:]
    block = own_ref.shape[0]
    for q, out in enumerate([own_ref] + outs):
        both = even_ref[(q + 1) * block : (q + 2) * block, :]
        both = both + other_ref[q * block : (q + 1) * block, :].astype(F32)
        out[:block, :] = both.astype(out.dtype)
        if half and q:
            out[block:, :] = half[0][...]


def rest_sums(even, other, block, *half):
    feat = even.shape[1]
    more = half[0].shape[0] if half else 0
    n_out = other.shape[0] // block - 1
    shapes = [jax.ShapeDtypeStruct((block, feat), F32)]
    shapes += [jax.ShapeDtypeStruct((block + more, feat), BF16)] * n_out
    return pl.pallas_call(
        functools.partial(rest_sum_kernel, len(half)),
        out_shape=shapes,
        in_specs=[vmem()] * (2 + len(half)),
        out_specs=[vmem()] * len(shapes),
        compiler_params=params(),
        cost_estimate=pl.CostEstimate(flops=other.size, bytes_accessed=other.size * 8, transcendentals=0),
    )(even, other, *half)


def total(values):
    values = [value.astype(F32) for value in values]
    if len(values) == 2:
        return values[0] + values[1]
    mine, across, one, other = values
    return (mine + across) + (one + other)


def layer_kernel(n_parts, *refs):
    parts, (weight_ref, cotangent_ref, pair_ref) = refs[:n_parts], refs[n_parts:]
    block = cotangent_ref.shape[0]
    agg = total([part[...] for part in parts]).astype(BF16)
    pre = jnp.dot(agg, weight_ref[...], preferred_element_type=F32)
    sig = 1.0 / (1.0 + jnp.exp(-pre))
    dpre = cotangent_ref[...].astype(F32) * sig * (1.0 + pre * (1.0 - sig))
    pair_ref[:block, :] = agg
    pair_ref[block:, :] = dpre.astype(BF16)


def layer(parts, weight, cotangent):
    block, feat = cotangent.shape
    return pl.pallas_call(
        functools.partial(layer_kernel, len(parts)),
        out_shape=jax.ShapeDtypeStruct((2 * block, feat), BF16),
        in_specs=[vmem()] * (len(parts) + 2),
        out_specs=vmem(),
        compiler_params=params(),
        cost_estimate=pl.CostEstimate(
            flops=2 * block * feat * feat, bytes_accessed=block * feat * 16, transcendentals=block * feat
        ),
    )(*parts, weight, cotangent)


def activation_kernel(pair_ref, weight_ref, out_ref):
    pre = jnp.dot(pair_ref[: out_ref.shape[0], :], weight_ref[...], preferred_element_type=F32)
    out_ref[...] = (pre / (1.0 + jnp.exp(-pre))).astype(out_ref.dtype)


def layer_output(pair, weight):
    shape = (pair.shape[0] // 2, pair.shape[1])
    return pl.pallas_call(
        activation_kernel,
        out_shape=jax.ShapeDtypeStruct(shape, BF16),
        in_specs=[vmem()] * 2,
        out_specs=vmem(),
        compiler_params=params(),
        cost_estimate=pl.CostEstimate(
            flops=pair.size * shape[1], bytes_accessed=pair.size * 4, transcendentals=pair.size // 2
        ),
    )(pair, weight)


def in_order(pairs, one, two):
    mine = lax.axis_index("rep")
    flip = (mine ^ one) > (mine ^ two)
    first, second = pairs[one][...], pairs[two][...]
    return jnp.where(flip, second, first), jnp.where(flip, first, second)


def pair_kernel(scale, order, groups, dense_ref, *refs):
    pairs = dict(zip(order, refs))
    first_ref, keep_ref = refs[len(order) :]
    block = pairs[0].shape[0] // 2
    dpre = jnp.concatenate([pairs[d][block:, :] for d in order], axis=0)
    rows = dense_ref.shape[0] // 2
    first = jnp.dot(dense_ref[rows : rows + block, :], dpre, preferred_element_type=F32)
    first_ref[:block, :] = first.astype(BF16)
    half = first_ref.shape[1] // 2
    upper = lower = 0.0
    for one, two in groups:
        low, high = in_order(pairs, one, two)
        agg = jnp.concatenate([low[:block, :], high[:block, :]], axis=0)
        dpre = jnp.concatenate([low[block:, :], high[block:, :]], axis=0)
        upper = upper + lax.dot_general(agg[:, :half], dpre, ROWS, preferred_element_type=F32)
        lower = lower + lax.dot_general(agg[:, half:], dpre, ROWS, preferred_element_type=F32)
    upper, lower = upper * scale, lower * scale
    is_first = lax.axis_index("blk") % 2 == 0
    first_ref[block:, :] = jnp.where(is_first, lower, upper).astype(BF16)
    keep_ref[...] = jnp.where(is_first, upper, lower)


def apply_pairs(dense, pairs, order, scale):
    feat = pairs[0].shape[1]
    block, half = pairs[0].shape[0] // 2, feat // 2
    groups = [(d, d + len(order) // 2) for d in range(len(order) // 2)]
    shapes = ((block + half, BF16), (half, F32))
    return pl.pallas_call(
        functools.partial(pair_kernel, scale, order, groups),
        out_shape=[jax.ShapeDtypeStruct((n, feat), t) for n, t in shapes],
        in_specs=[vmem()] * (1 + len(pairs)),
        out_specs=[vmem()] * 2,
        compiler_params=params(),
        cost_estimate=pl.CostEstimate(
            flops=6 * len(pairs) * block * feat * feat, bytes_accessed=dense.size, transcendentals=0
        ),
    )(dense, *pairs)


def half_kernel(half_ref, *refs):
    parts, out_ref = refs[:-1], refs[-1]
    more = half_ref.shape[0]
    out_ref[...] = total([half_ref[...]] + [part[-more:, :] for part in parts]).astype(out_ref.dtype)


def half_sum(half, parts):
    return pl.pallas_call(
        half_kernel,
        out_shape=jax.ShapeDtypeStruct(half.shape, BF16),
        in_specs=[vmem()] * (1 + len(parts)),
        out_specs=vmem(),
        compiler_params=params(),
        cost_estimate=pl.CostEstimate(flops=half.size * 4, bytes_accessed=half.size * 12, transcendentals=0),
    )(half, *parts)


def last_kernel(weight_ref, own_ref, *refs):
    parts, out_ref = refs[:-1], refs[-1]
    block = own_ref.shape[0]
    rows = total([own_ref[...]] + [part[:block, :] for part in parts]).astype(BF16)
    out_ref[...] = lax.dot_general(
        rows, weight_ref[...], (((1,), (1,)), ((), ())), preferred_element_type=F32
    ).astype(out_ref.dtype)


def last_product(weight, own, parts):
    return pl.pallas_call(
        last_kernel,
        out_shape=jax.ShapeDtypeStruct(own.shape, BF16),
        in_specs=[vmem()] * (2 + len(parts)),
        out_specs=vmem(),
        compiler_params=params(),
        cost_estimate=pl.CostEstimate(flops=2 * own.size * own.shape[1], bytes_accessed=own.size * 12, transcendentals=0),
    )(weight, own, *parts)


def gather(value, order):
    return [value] + [send(value, "rep", at(d)) for d in order]


def join(mine):
    other = send(mine, "blk", at(1))
    is_first = lax.axis_index("blk") % 2 == 0
    return jnp.where(
        is_first, jnp.concatenate([mine, other], axis=0), jnp.concatenate([other, mine], axis=0)
    )


def shards_direct(features, weight, cotangent, rows, counts, tiles):
    block = features.shape[0]
    slabs, subs = lax.axis_size("blk"), lax.axis_size("rep")
    far, near = far_steps(slabs), sub_order(subs)
    node_count = block * slabs * subs
    even = far[:1] + [at(0)] + far[1:]
    odd = [lambda i, step=step: step(i) ^ 1 for step in even]
    dense = dense_adjacency(even + odd, [0] + near, rows, counts, tiles)

    pieces, dense = lax.optimization_barrier((gather(features, near), dense))
    other = send(apply_first(dense, pieces), "blk", at(1))
    rest, mine = apply_rest(dense, pieces, block)
    rest, other = lax.optimization_barrier((rest, other))
    (first,) = first_sum(mine, other, block)
    own, *sums = rest_sums(mine, send(rest, "blk", at(1)), block)
    parts = [send(value, "blk", step) for value, step in zip([first] + sums, far)]

    pair = layer([own] + parts, weight, cotangent)
    pairs = gather(pair, near)
    activation = layer_output(pair, weight)
    pairs, activation = lax.optimization_barrier((pairs, activation))
    first, keep = apply_pairs(dense, pairs, [0] + near, 1.0 / math.sqrt(node_count))
    other = send(first, "blk", at(1))
    rest, mine = apply_rest(dense, pairs, block)
    rest, other = lax.optimization_barrier((rest, other))
    first, half = first_sum(mine, other, block, keep)
    own, *sums = rest_sums(mine, send(rest, "blk", at(1)), block, half)
    parts = [send(value, "blk", step) for value, step in zip([first] + sums, far)]
    grad = join(half_sum(half, parts)).astype(F32)
    return activation, grad, last_product(weight, own, parts)


def add_tile(running, column_block, node_slab, tiles, slot_rows, slot_counts):
    block_size = node_slab.shape[0]
    tile_now = lax.dynamic_index_in_dim(tiles, column_block, 0, keepdims=False)
    rows_now = lax.dynamic_index_in_dim(slot_rows, column_block, 0, keepdims=False)
    count_now = lax.dynamic_index_in_dim(slot_counts, column_block, 0, keepdims=False)

    def one_slot(slot_index, carried):
        weights_now = lax.dynamic_slice_in_dim(tile_now, slot_index * block_size, block_size, 1)
        product = jnp.dot(weights_now, node_slab, preferred_element_type=F32)
        first_row = rows_now[slot_index] * block_size
        current = lax.dynamic_slice_in_dim(carried, first_row, block_size, 0)
        return lax.dynamic_update_slice_in_dim(carried, current + product, first_row, 0)

    return lax.fori_loop(0, count_now, one_slot, running)


def aggregate(node_slab, tiles, slot_rows, slot_counts):
    block_size = node_slab.shape[0]
    running = jnp.zeros((block_size * lax.axis_size("rep"), node_slab.shape[1]), F32)
    piece = lax.all_gather(node_slab, "blk", axis=0, tiled=True)
    piece_count = piece.shape[0] // block_size

    def one_piece(inner, running_now):
        slab_now = lax.dynamic_slice_in_dim(piece, inner * block_size, block_size, 0)
        return add_tile(running_now, inner, slab_now, tiles, slot_rows, slot_counts)

    total = lax.fori_loop(0, piece_count, one_piece, running)
    return lax.psum_scatter(total.astype(BF16), "rep", scatter_dimension=0, tiled=True)


def shards_general(features, weight, cotangent, rows, counts, tiles):
    agg = aggregate(features, tiles, rows, counts)
    pre = jnp.dot(agg, weight, preferred_element_type=F32)
    sig = jax.nn.sigmoid(pre)
    activation = (pre * sig).astype(BF16)
    dpre = (cotangent.astype(F32) * sig * (1.0 + pre * (1.0 - sig))).astype(BF16)
    local_grad = lax.dot_general(agg, dpre, (((0,), (0,)), ((), ())), preferred_element_type=F32)
    node_count = features.shape[0] * lax.axis_size("blk") * lax.axis_size("rep")
    grad_weight = lax.psum(local_grad, ("blk", "rep")) / math.sqrt(node_count)
    back = lax.dot_general(dpre, weight, (((1,), (1,)), ((), ())), preferred_element_type=F32)
    return activation, grad_weight, aggregate(back.astype(BF16), tiles, rows, counts)


def shards(features, weight, cotangent, block_rows, block_counts, block_values):
    tiles = block_values[0, :, 0]
    rows = block_rows[0, :, 0]
    counts = block_counts[0, :, 0]
    sizes = lax.axis_size("blk"), lax.axis_size("rep")
    direct = sizes[0] in (4, 8) and sizes[1] in (2, 4)
    return (shards_direct if direct else shards_general)(
        features, weight, cotangent, rows, counts, tiles
    )


def solution(mesh):
    placed = (
        P(("blk", "rep"), None),
        P(),
        P(("blk", "rep"), None),
        P("blk", None, "rep", None),
        P("blk", None, "rep"),
        P("blk", None, "rep", None, None),
    )
    return jax.shard_map(
        shards,
        mesh=mesh,
        in_specs=placed,
        out_specs=(P(("blk", "rep"), None), P(), P(("blk", "rep"), None)),
        check_vma=False,
    )
```

```python
import functools
import math

import jax
import jax.numpy as jnp
from jax import lax
from jax.experimental import pallas as pl
from jax.experimental.pallas import tpu as pltpu
from jax.sharding import PartitionSpec as P

F32 = jnp.float32
BF16 = jnp.bfloat16
ROWS = (((0,), (0,)), ((), ()))
VMEM_LIMIT = 8 * 1024 * 1024


def vmem():
    return pl.BlockSpec(memory_space=pltpu.VMEM)


def smem():
    return pl.BlockSpec(memory_space=pltpu.SMEM)


def params():
    return pltpu.CompilerParams(vmem_limit_bytes=VMEM_LIMIT)


def send(value, axis, step):
    return lax.ppermute(value, axis, [(i, step(i)) for i in range(lax.axis_size(axis))])


def at(distance):
    return lambda i: i ^ distance


def far_steps(slabs):
    if slabs == 8:
        return [at(6), at(2), at(4)]
    return [at(2)]


def sub_order(subs):
    return [2, 1, 3] if subs == 4 else [1]


def dense_kernel(steps, subs, rows_ref, counts_ref, tiles_ref, out_ref):
    me, mine = lax.axis_index("blk"), lax.axis_index("rep")
    block = tiles_ref.shape[1]
    slots = tiles_ref.shape[2] // block
    for q, step in enumerate(steps):
        slab = step(me)
        tile = tiles_ref[slab]
        turned = [tile[:, k * block : (k + 1) * block].T for k in range(slots)]
        places = [
            jnp.where(k < counts_ref[slab], rows_ref[slab, k] ^ mine, -1) for k in range(slots)
        ]
        for b, sub in enumerate(subs):
            value = jnp.zeros((block, block), tile.dtype)
            for k in range(slots):
                value = jnp.where(places[k] == sub, turned[k], value)
            out_ref[q * block : (q + 1) * block, b * block : (b + 1) * block] = value


def dense_adjacency(steps, subs, rows, counts, tiles):
    block = tiles.shape[1]
    shape = (len(steps) * block, len(subs) * block)
    return pl.pallas_call(
        functools.partial(dense_kernel, steps, subs),
        out_shape=jax.ShapeDtypeStruct(shape, tiles.dtype),
        in_specs=[smem(), smem(), vmem()],
        out_specs=vmem(),
        compiler_params=params(),
        cost_estimate=pl.CostEstimate(flops=0, bytes_accessed=4 * tiles.size * 2, transcendentals=0),
    )(rows, counts, tiles)


def first_kernel(order, dense_ref, *refs):
    nodes = jnp.concatenate([refs[k][...] for k in order], axis=0)
    out_ref = refs[-1]
    half = dense_ref.shape[0] // 2
    rows = dense_ref[half : half + out_ref.shape[0], :]
    out_ref[...] = jnp.dot(rows, nodes, preferred_element_type=F32).astype(out_ref.dtype)


def apply_first(dense, pieces, order):
    shape = pieces[0].shape
    return pl.pallas_call(
        functools.partial(first_kernel, order),
        out_shape=jax.ShapeDtypeStruct(shape, BF16),
        in_specs=[vmem()] * (1 + len(pieces)),
        out_specs=vmem(),
        compiler_params=params(),
        cost_estimate=pl.CostEstimate(
            flops=2 * dense.shape[1] * shape[0] * shape[1], bytes_accessed=dense.size // 4, transcendentals=0
        ),
    )(dense, *pieces)


def rest_kernel(block, order, dense_ref, *refs):
    nodes = jnp.concatenate([refs[k][-block:, :] for k in order], axis=0)
    odd_ref, even_ref = refs[len(order) :]
    half = dense_ref.shape[0] // 2
    rows = dense_ref[dense_ref.shape[0] - odd_ref.shape[0] :, :]
    odd_ref[...] = jnp.dot(rows, nodes, preferred_element_type=F32).astype(odd_ref.dtype)
    even_ref[...] = jnp.dot(dense_ref[:half, :], nodes, preferred_element_type=F32)


def apply_rest(dense, pieces, order, block):
    rows, feat = dense.shape[0] // 2, pieces[0].shape[1]
    return pl.pallas_call(
        functools.partial(rest_kernel, block, order),
        out_shape=[jax.ShapeDtypeStruct((rows - block, feat), BF16), jax.ShapeDtypeStruct((rows, feat), F32)],
        in_specs=[vmem()] * (1 + len(pieces)),
        out_specs=[vmem()] * 2,
        compiler_params=params(),
        cost_estimate=pl.CostEstimate(
            flops=2 * dense.size * feat, bytes_accessed=2 * dense.size, transcendentals=0
        ),
    )(dense, *pieces)


def first_sum_kernel(even_ref, other_ref, *refs):
    block = even_ref.shape[0]
    if len(refs) == 1:
        refs[0][...] = (even_ref[...] + other_ref[...].astype(F32)).astype(BF16)
        return
    keep_ref, out_ref, half_ref = refs
    out_ref[:block, :] = (even_ref[...] + other_ref[:block, :].astype(F32)).astype(BF16)
    half = (keep_ref[...] + other_ref[block:, :].astype(F32)).astype(BF16)
    out_ref[block:, :] = half
    half_ref[...] = half


def first_sum(even, other, block, *keep):
    shapes = [jax.ShapeDtypeStruct(other.shape, BF16)]
    shapes += [jax.ShapeDtypeStruct(half.shape, BF16) for half in keep]
    top = pl.BlockSpec((block, even.shape[1]), lambda i: (0, 0))
    return pl.pallas_call(
        first_sum_kernel,
        grid=(1,),
        out_shape=shapes,
        in_specs=[top] + [vmem()] * (1 + len(keep)),
        out_specs=[vmem()] * len(shapes),
        compiler_params=params(),
        cost_estimate=pl.CostEstimate(flops=other.size, bytes_accessed=other.size * 8, transcendentals=0),
    )(even, other, *keep)


def rest_sum_kernel(n_half, even_ref, other_ref, *refs):
    half, (own_ref, *outs) = refs[:n_half], refs[n_half:]
    block = own_ref.shape[0]
    for q, out in enumerate([own_ref] + outs):
        both = even_ref[(q + 1) * block : (q + 2) * block, :]
        both = both + other_ref[q * block : (q + 1) * block, :].astype(F32)
        out[:block, :] = both.astype(out.dtype)
        if half and q:
            out[block:, :] = half[0][...]


def rest_sums(even, other, block, *half):
    feat = even.shape[1]
    more = half[0].shape[0] if half else 0
    n_out = other.shape[0] // block - 1
    shapes = [jax.ShapeDtypeStruct((block, feat), F32)]
    shapes += [jax.ShapeDtypeStruct((block + more, feat), BF16)] * n_out
    return pl.pallas_call(
        functools.partial(rest_sum_kernel, len(half)),
        out_shape=shapes,
        in_specs=[vmem()] * (2 + len(half)),
        out_specs=[vmem()] * len(shapes),
        compiler_params=params(),
        cost_estimate=pl.CostEstimate(flops=other.size, bytes_accessed=other.size * 8, transcendentals=0),
    )(even, other, *half)


def total(values):
    values = [value.astype(F32) for value in values]
    if len(values) == 2:
        return values[0] + values[1]
    mine, across, one, other = values
    return (mine + across) + (one + other)


def layer_kernel(n_parts, *refs):
    parts, (weight_ref, cotangent_ref, pair_ref) = refs[:n_parts], refs[n_parts:]
    block = cotangent_ref.shape[0]
    agg = total([part[...] for part in parts]).astype(BF16)
    pre = jnp.dot(agg, weight_ref[...], preferred_element_type=F32)
    sig = 1.0 / (1.0 + jnp.exp(-pre))
    dpre = cotangent_ref[...].astype(F32) * sig * (1.0 + pre * (1.0 - sig))
    pair_ref[:block, :] = agg
    pair_ref[block:, :] = dpre.astype(BF16)


def layer(parts, weight, cotangent):
    block, feat = cotangent.shape
    return pl.pallas_call(
        functools.partial(layer_kernel, len(parts)),
        out_shape=jax.ShapeDtypeStruct((2 * block, feat), BF16),
        in_specs=[vmem()] * (len(parts) + 2),
        out_specs=vmem(),
        compiler_params=params(),
        cost_estimate=pl.CostEstimate(
            flops=2 * block * feat * feat, bytes_accessed=block * feat * 16, transcendentals=block * feat
        ),
    )(*parts, weight, cotangent)


def activation_kernel(pair_ref, weight_ref, out_ref):
    pre = jnp.dot(pair_ref[: out_ref.shape[0], :], weight_ref[...], preferred_element_type=F32)
    out_ref[...] = (pre / (1.0 + jnp.exp(-pre))).astype(out_ref.dtype)


def layer_output(pair, weight):
    shape = (pair.shape[0] // 2, pair.shape[1])
    return pl.pallas_call(
        activation_kernel,
        out_shape=jax.ShapeDtypeStruct(shape, BF16),
        in_specs=[vmem()] * 2,
        out_specs=vmem(),
        compiler_params=params(),
        cost_estimate=pl.CostEstimate(
            flops=pair.size * shape[1], bytes_accessed=pair.size * 4, transcendentals=pair.size // 2
        ),
    )(pair, weight)


def in_order(pairs, one, two):
    mine = lax.axis_index("rep")
    flip = (mine ^ one) > (mine ^ two)
    first, second = pairs[one][...], pairs[two][...]
    return jnp.where(flip, second, first), jnp.where(flip, first, second)


def pair_kernel(scale, order, groups, dense_ref, *refs):
    pairs = dict(zip(order, refs))
    first_ref, keep_ref = refs[len(order) :]
    block = pairs[0].shape[0] // 2
    dpre = jnp.concatenate([pairs[d][block:, :] for d in order], axis=0)
    rows = dense_ref.shape[0] // 2
    first = jnp.dot(dense_ref[rows : rows + block, :], dpre, preferred_element_type=F32)
    first_ref[:block, :] = first.astype(BF16)
    half = first_ref.shape[1] // 2
    upper = lower = 0.0
    for one, two in groups:
        low, high = in_order(pairs, one, two)
        agg = jnp.concatenate([low[:block, :], high[:block, :]], axis=0)
        dpre = jnp.concatenate([low[block:, :], high[block:, :]], axis=0)
        upper = upper + lax.dot_general(agg[:, :half], dpre, ROWS, preferred_element_type=F32)
        lower = lower + lax.dot_general(agg[:, half:], dpre, ROWS, preferred_element_type=F32)
    upper, lower = upper * scale, lower * scale
    is_first = lax.axis_index("blk") % 2 == 0
    first_ref[block:, :] = jnp.where(is_first, lower, upper).astype(BF16)
    keep_ref[...] = jnp.where(is_first, upper, lower)


def apply_pairs(dense, pairs, order, scale):
    feat = pairs[0].shape[1]
    block, half = pairs[0].shape[0] // 2, feat // 2
    groups = [(d, d + len(order) // 2) for d in range(len(order) // 2)]
    shapes = ((block + half, BF16), (half, F32))
    return pl.pallas_call(
        functools.partial(pair_kernel, scale, order, groups),
        out_shape=[jax.ShapeDtypeStruct((n, feat), t) for n, t in shapes],
        in_specs=[vmem()] * (1 + len(pairs)),
        out_specs=[vmem()] * 2,
        compiler_params=params(),
        cost_estimate=pl.CostEstimate(
            flops=6 * len(pairs) * block * feat * feat, bytes_accessed=dense.size, transcendentals=0
        ),
    )(dense, *pairs)


def half_kernel(half_ref, *refs):
    parts, out_ref = refs[:-1], refs[-1]
    more = half_ref.shape[0]
    out_ref[...] = total([half_ref[...]] + [part[-more:, :] for part in parts]).astype(out_ref.dtype)


def half_sum(half, parts):
    return pl.pallas_call(
        half_kernel,
        out_shape=jax.ShapeDtypeStruct(half.shape, BF16),
        in_specs=[vmem()] * (1 + len(parts)),
        out_specs=vmem(),
        compiler_params=params(),
        cost_estimate=pl.CostEstimate(flops=half.size * 4, bytes_accessed=half.size * 12, transcendentals=0),
    )(half, *parts)


def last_kernel(weight_ref, own_ref, *refs):
    parts, out_ref = refs[:-1], refs[-1]
    block = own_ref.shape[0]
    rows = total([own_ref[...]] + [part[:block, :] for part in parts]).astype(BF16)
    out_ref[...] = lax.dot_general(
        rows, weight_ref[...], (((1,), (1,)), ((), ())), preferred_element_type=F32
    ).astype(out_ref.dtype)


def last_product(weight, own, parts):
    return pl.pallas_call(
        last_kernel,
        out_shape=jax.ShapeDtypeStruct(own.shape, BF16),
        in_specs=[vmem()] * (2 + len(parts)),
        out_specs=vmem(),
        compiler_params=params(),
        cost_estimate=pl.CostEstimate(flops=2 * own.size * own.shape[1], bytes_accessed=own.size * 12, transcendentals=0),
    )(weight, own, *parts)


def gather(value, order):
    return [value] + [send(value, "rep", at(d)) for d in order]


def join(mine):
    other = send(mine, "blk", at(1))
    is_first = lax.axis_index("blk") % 2 == 0
    return jnp.where(
        is_first, jnp.concatenate([mine, other], axis=0), jnp.concatenate([other, mine], axis=0)
    )


def shards_direct(features, weight, cotangent, rows, counts, tiles):
    block = features.shape[0]
    slabs, subs = lax.axis_size("blk"), lax.axis_size("rep")
    far, near, early = far_steps(slabs), sub_order(subs), [3, 2, 1] if subs == 4 else [1]
    straight = list(range(subs))
    order = [([0] + early).index(d) for d in [0] + near]
    node_count = block * slabs * subs
    even = far[:1] + [at(0)] + far[1:]
    odd = [lambda i, step=step: step(i) ^ 1 for step in even]
    dense = dense_adjacency(even + odd, [0] + near, rows, counts, tiles)

    pieces, dense = lax.optimization_barrier((gather(features, early), dense))
    other = send(apply_first(dense, pieces, order), "blk", at(1))
    rest, mine = apply_rest(dense, pieces, order, block)
    rest, other = lax.optimization_barrier((rest, other))
    (first,) = first_sum(mine, other, block)
    own, *sums = rest_sums(mine, send(rest, "blk", at(1)), block)
    parts = [send(value, "blk", step) for value, step in zip([first] + sums, far)]

    pair = layer([own] + parts, weight, cotangent)
    pairs = gather(pair, near)
    activation = layer_output(pair, weight)
    pairs, activation = lax.optimization_barrier((pairs, activation))
    first, keep = apply_pairs(dense, pairs, [0] + near, 1.0 / math.sqrt(node_count))
    other = send(first, "blk", at(1))
    rest, mine = apply_rest(dense, pairs, straight, block)
    rest, other = lax.optimization_barrier((rest, other))
    first, half = first_sum(mine, other, block, keep)
    own, *sums = rest_sums(mine, send(rest, "blk", at(1)), block, half)
    parts = [send(value, "blk", step) for value, step in zip([first] + sums, far)]
    grad = join(half_sum(half, parts)).astype(F32)
    return activation, grad, last_product(weight, own, parts)


def add_tile(running, column_block, node_slab, tiles, slot_rows, slot_counts):
    block_size = node_slab.shape[0]
    tile_now = lax.dynamic_index_in_dim(tiles, column_block, 0, keepdims=False)
    rows_now = lax.dynamic_index_in_dim(slot_rows, column_block, 0, keepdims=False)
    count_now = lax.dynamic_index_in_dim(slot_counts, column_block, 0, keepdims=False)

    def one_slot(slot_index, carried):
        weights_now = lax.dynamic_slice_in_dim(tile_now, slot_index * block_size, block_size, 1)
        product = jnp.dot(weights_now, node_slab, preferred_element_type=F32)
        first_row = rows_now[slot_index] * block_size
        current = lax.dynamic_slice_in_dim(carried, first_row, block_size, 0)
        return lax.dynamic_update_slice_in_dim(carried, current + product, first_row, 0)

    return lax.fori_loop(0, count_now, one_slot, running)


def aggregate(node_slab, tiles, slot_rows, slot_counts):
    block_size = node_slab.shape[0]
    running = jnp.zeros((block_size * lax.axis_size("rep"), node_slab.shape[1]), F32)
    piece = lax.all_gather(node_slab, "blk", axis=0, tiled=True)
    piece_count = piece.shape[0] // block_size

    def one_piece(inner, running_now):
        slab_now = lax.dynamic_slice_in_dim(piece, inner * block_size, block_size, 0)
        return add_tile(running_now, inner, slab_now, tiles, slot_rows, slot_counts)

    total = lax.fori_loop(0, piece_count, one_piece, running)
    return lax.psum_scatter(total.astype(BF16), "rep", scatter_dimension=0, tiled=True)


def shards_general(features, weight, cotangent, rows, counts, tiles):
    agg = aggregate(features, tiles, rows, counts)
    pre = jnp.dot(agg, weight, preferred_element_type=F32)
    sig = jax.nn.sigmoid(pre)
    activation = (pre * sig).astype(BF16)
    dpre = (cotangent.astype(F32) * sig * (1.0 + pre * (1.0 - sig))).astype(BF16)
    local_grad = lax.dot_general(agg, dpre, (((0,), (0,)), ((), ())), preferred_element_type=F32)
    node_count = features.shape[0] * lax.axis_size("blk") * lax.axis_size("rep")
    grad_weight = lax.psum(local_grad, ("blk", "rep")) / math.sqrt(node_count)
    back = lax.dot_general(dpre, weight, (((1,), (1,)), ((), ())), preferred_element_type=F32)
    return activation, grad_weight, aggregate(back.astype(BF16), tiles, rows, counts)


def shards(features, weight, cotangent, block_rows, block_counts, block_values):
    tiles = block_values[0, :, 0]
    rows = block_rows[0, :, 0]
    counts = block_counts[0, :, 0]
    sizes = lax.axis_size("blk"), lax.axis_size("rep")
    direct = sizes[0] in (4, 8) and sizes[1] in (2, 4)
    return (shards_direct if direct else shards_general)(
        features, weight, cotangent, rows, counts, tiles
    )


def solution(mesh):
    placed = (
        P(("blk", "rep"), None),
        P(),
        P(("blk", "rep"), None),
        P("blk", None, "rep", None),
        P("blk", None, "rep"),
        P("blk", None, "rep", None, None),
    )
    return jax.shard_map(
        shards,
        mesh=mesh,
        in_specs=placed,
        out_specs=(P(("blk", "rep"), None), P(), P(("blk", "rep"), None)),
        check_vma=False,
    )
```

```python
import functools
import math

import jax
import jax.numpy as jnp
from jax import lax
from jax.experimental import pallas as pl
from jax.experimental.pallas import tpu as pltpu
from jax.sharding import PartitionSpec as P

F32 = jnp.float32
BF16 = jnp.bfloat16
ROWS = (((0,), (0,)), ((), ()))
VMEM_LIMIT = 8 * 1024 * 1024


def vmem():
    return pl.BlockSpec(memory_space=pltpu.VMEM)


def smem():
    return pl.BlockSpec(memory_space=pltpu.SMEM)


def params():
    return pltpu.CompilerParams(vmem_limit_bytes=VMEM_LIMIT)


def send(value, axis, step):
    return lax.ppermute(value, axis, [(i, step(i)) for i in range(lax.axis_size(axis))])


def at(distance):
    return lambda i: i ^ distance


def far_steps(slabs):
    if slabs == 8:
        return [at(6), at(2), at(4)]
    return [at(2)]


def sub_order(subs):
    return [1, 3, 2] if subs == 4 else [1]


def dense_kernel(steps, subs, rows_ref, counts_ref, tiles_ref, out_ref):
    me, mine = lax.axis_index("blk"), lax.axis_index("rep")
    block = tiles_ref.shape[1]
    slots = tiles_ref.shape[2] // block
    for q, step in enumerate(steps):
        slab = step(me)
        tile = tiles_ref[slab]
        turned = [tile[:, k * block : (k + 1) * block].T for k in range(slots)]
        places = [
            jnp.where(k < counts_ref[slab], rows_ref[slab, k] ^ mine, -1) for k in range(slots)
        ]
        for b, sub in enumerate(subs):
            value = jnp.zeros((block, block), tile.dtype)
            for k in range(slots):
                value = jnp.where(places[k] == sub, turned[k], value)
            out_ref[q * block : (q + 1) * block, b * block : (b + 1) * block] = value


def dense_adjacency(steps, subs, rows, counts, tiles):
    block = tiles.shape[1]
    shape = (len(steps) * block, len(subs) * block)
    return pl.pallas_call(
        functools.partial(dense_kernel, steps, subs),
        out_shape=jax.ShapeDtypeStruct(shape, tiles.dtype),
        in_specs=[smem(), smem(), vmem()],
        out_specs=vmem(),
        compiler_params=params(),
        cost_estimate=pl.CostEstimate(flops=0, bytes_accessed=4 * tiles.size * 2, transcendentals=0),
    )(rows, counts, tiles)


def first_kernel(order, dense_ref, *refs):
    nodes = jnp.concatenate([refs[k][...] for k in order], axis=0)
    out_ref = refs[-1]
    half = dense_ref.shape[0] // 2
    rows = dense_ref[half : half + out_ref.shape[0], :]
    out_ref[...] = jnp.dot(rows, nodes, preferred_element_type=F32).astype(out_ref.dtype)


def apply_first(dense, pieces, order):
    shape = pieces[0].shape
    return pl.pallas_call(
        functools.partial(first_kernel, order),
        out_shape=jax.ShapeDtypeStruct(shape, BF16),
        in_specs=[vmem()] * (1 + len(pieces)),
        out_specs=vmem(),
        compiler_params=params(),
        cost_estimate=pl.CostEstimate(
            flops=2 * dense.shape[1] * shape[0] * shape[1], bytes_accessed=dense.size // 4, transcendentals=0
        ),
    )(dense, *pieces)


def rest_kernel(block, order, dense_ref, *refs):
    nodes = jnp.concatenate([refs[k][-block:, :] for k in order], axis=0)
    odd_ref, even_ref = refs[len(order) :]
    half = dense_ref.shape[0] // 2
    rows = dense_ref[dense_ref.shape[0] - odd_ref.shape[0] :, :]
    odd_ref[...] = jnp.dot(rows, nodes, preferred_element_type=F32).astype(odd_ref.dtype)
    even_ref[...] = jnp.dot(dense_ref[:half, :], nodes, preferred_element_type=F32)


def apply_rest(dense, pieces, order, block):
    rows, feat = dense.shape[0] // 2, pieces[0].shape[1]
    return pl.pallas_call(
        functools.partial(rest_kernel, block, order),
        out_shape=[jax.ShapeDtypeStruct((rows - block, feat), BF16), jax.ShapeDtypeStruct((rows, feat), F32)],
        in_specs=[vmem()] * (1 + len(pieces)),
        out_specs=[vmem()] * 2,
        compiler_params=params(),
        cost_estimate=pl.CostEstimate(
            flops=2 * dense.size * feat, bytes_accessed=2 * dense.size, transcendentals=0
        ),
    )(dense, *pieces)


def first_sum_kernel(even_ref, other_ref, *refs):
    block = even_ref.shape[0]
    if len(refs) == 1:
        refs[0][...] = (even_ref[...] + other_ref[...].astype(F32)).astype(BF16)
        return
    keep_ref, out_ref, half_ref = refs
    out_ref[:block, :] = (even_ref[...] + other_ref[:block, :].astype(F32)).astype(BF16)
    half = (keep_ref[...] + other_ref[block:, :].astype(F32)).astype(BF16)
    out_ref[block:, :] = half
    half_ref[...] = half


def first_sum(even, other, block, *keep):
    shapes = [jax.ShapeDtypeStruct(other.shape, BF16)]
    shapes += [jax.ShapeDtypeStruct(half.shape, BF16) for half in keep]
    top = pl.BlockSpec((block, even.shape[1]), lambda i: (0, 0))
    return pl.pallas_call(
        first_sum_kernel,
        grid=(1,),
        out_shape=shapes,
        in_specs=[top] + [vmem()] * (1 + len(keep)),
        out_specs=[vmem()] * len(shapes),
        compiler_params=params(),
        cost_estimate=pl.CostEstimate(flops=other.size, bytes_accessed=other.size * 8, transcendentals=0),
    )(even, other, *keep)


def rest_sum_kernel(n_half, even_ref, other_ref, *refs):
    half, (own_ref, *outs) = refs[:n_half], refs[n_half:]
    block = own_ref.shape[0]
    for q, out in enumerate([own_ref] + outs):
        both = even_ref[(q + 1) * block : (q + 2) * block, :]
        both = both + other_ref[q * block : (q + 1) * block, :].astype(F32)
        out[:block, :] = both.astype(out.dtype)
        if half and q:
            out[block:, :] = half[0][...]


def rest_sums(even, other, block, *half):
    feat = even.shape[1]
    more = half[0].shape[0] if half else 0
    n_out = other.shape[0] // block - 1
    shapes = [jax.ShapeDtypeStruct((block, feat), F32)]
    shapes += [jax.ShapeDtypeStruct((block + more, feat), BF16)] * n_out
    return pl.pallas_call(
        functools.partial(rest_sum_kernel, len(half)),
        out_shape=shapes,
        in_specs=[vmem()] * (2 + len(half)),
        out_specs=[vmem()] * len(shapes),
        compiler_params=params(),
        cost_estimate=pl.CostEstimate(flops=other.size, bytes_accessed=other.size * 8, transcendentals=0),
    )(even, other, *half)


def total(values):
    values = [value.astype(F32) for value in values]
    if len(values) == 2:
        return values[0] + values[1]
    mine, across, one, other = values
    return (mine + across) + (one + other)


def layer_kernel(n_parts, *refs):
    parts, (weight_ref, cotangent_ref, pair_ref) = refs[:n_parts], refs[n_parts:]
    block = cotangent_ref.shape[0]
    agg = total([part[...] for part in parts]).astype(BF16)
    pre = jnp.dot(agg, weight_ref[...], preferred_element_type=F32)
    sig = 1.0 / (1.0 + jnp.exp(-pre))
    dpre = cotangent_ref[...].astype(F32) * sig * (1.0 + pre * (1.0 - sig))
    pair_ref[:block, :] = agg
    pair_ref[block:, :] = dpre.astype(BF16)


def layer(parts, weight, cotangent):
    block, feat = cotangent.shape
    return pl.pallas_call(
        functools.partial(layer_kernel, len(parts)),
        out_shape=jax.ShapeDtypeStruct((2 * block, feat), BF16),
        in_specs=[vmem()] * (len(parts) + 2),
        out_specs=vmem(),
        compiler_params=params(),
        cost_estimate=pl.CostEstimate(
            flops=2 * block * feat * feat, bytes_accessed=block * feat * 16, transcendentals=block * feat
        ),
    )(*parts, weight, cotangent)


def activation_kernel(pair_ref, weight_ref, out_ref):
    pre = jnp.dot(pair_ref[: out_ref.shape[0], :], weight_ref[...], preferred_element_type=F32)
    out_ref[...] = (pre / (1.0 + jnp.exp(-pre))).astype(out_ref.dtype)


def layer_output(pair, weight):
    shape = (pair.shape[0] // 2, pair.shape[1])
    return pl.pallas_call(
        activation_kernel,
        out_shape=jax.ShapeDtypeStruct(shape, BF16),
        in_specs=[vmem()] * 2,
        out_specs=vmem(),
        compiler_params=params(),
        cost_estimate=pl.CostEstimate(
            flops=pair.size * shape[1], bytes_accessed=pair.size * 4, transcendentals=pair.size // 2
        ),
    )(pair, weight)


def pair_terms(dense, distances, pairs):
    block = pairs[0].shape[0] // 2
    first = jnp.dot(
        dense, jnp.concatenate([pair[block:, :] for pair in pairs], axis=0), preferred_element_type=F32
    )
    if len(pairs) == 2:
        mine = lax.axis_index("rep")
        flip = (mine ^ distances[0]) > (mine ^ distances[1])
        one, two = pairs
        pairs = [jnp.where(flip, two, one), jnp.where(flip, one, two)]
    agg = jnp.concatenate([pair[:block, :] for pair in pairs], axis=0)
    dpre = jnp.concatenate([pair[block:, :] for pair in pairs], axis=0)
    return first, lax.dot_general(agg, dpre, ROWS, preferred_element_type=F32)


def early_kernel(distances, dense_ref, *refs):
    pairs, (first_ref, grad_ref) = refs[: len(distances)], refs[len(distances) :]
    block = first_ref.shape[0]
    rows = dense_ref.shape[0] // 2
    part = dense_ref[rows : rows + block, : len(pairs) * block]
    first_ref[...], grad_ref[...] = pair_terms(part, distances, [pair[...] for pair in pairs])


def late_kernel(scale, distances, dense_ref, early_ref, grad_ref, *refs):
    pairs, (first_ref, keep_ref) = refs[: len(distances)], refs[len(distances) :]
    block = early_ref.shape[0]
    rows, columns = dense_ref.shape[0] // 2, dense_ref.shape[1] - len(pairs) * block
    part = dense_ref[rows : rows + block, columns:]
    first, grad = pair_terms(part, distances, [pair[...] for pair in pairs])
    first_ref[:block, :] = (early_ref[...] + first).astype(BF16)
    grad = (grad_ref[...] + grad) * scale
    half = grad.shape[0] // 2
    upper, lower = grad[:half, :], grad[half:, :]
    is_first = lax.axis_index("blk") % 2 == 0
    first_ref[block:, :] = jnp.where(is_first, lower, upper).astype(BF16)
    keep_ref[...] = jnp.where(is_first, upper, lower)


def apply_early(dense, pairs, distances):
    block, feat = pairs[0].shape[0] // 2, pairs[0].shape[1]
    return pl.pallas_call(
        functools.partial(early_kernel, distances),
        out_shape=[jax.ShapeDtypeStruct((n, feat), F32) for n in (block, feat)],
        in_specs=[vmem()] * (1 + len(pairs)),
        out_specs=[vmem()] * 2,
        compiler_params=params(),
        cost_estimate=pl.CostEstimate(
            flops=6 * len(pairs) * block * feat * feat, bytes_accessed=dense.size, transcendentals=0
        ),
    )(dense, *pairs)


def apply_late(dense, early, pairs, distances, scale):
    feat = pairs[0].shape[1]
    block, half = pairs[0].shape[0] // 2, feat // 2
    shapes = ((block + half, BF16), (half, F32))
    return pl.pallas_call(
        functools.partial(late_kernel, scale, distances),
        out_shape=[jax.ShapeDtypeStruct((n, feat), t) for n, t in shapes],
        in_specs=[vmem()] * (3 + len(pairs)),
        out_specs=[vmem()] * 2,
        compiler_params=params(),
        cost_estimate=pl.CostEstimate(
            flops=6 * len(pairs) * block * feat * feat, bytes_accessed=dense.size, transcendentals=0
        ),
    )(dense, *early, *pairs)


def half_kernel(half_ref, *refs):
    parts, out_ref = refs[:-1], refs[-1]
    more = half_ref.shape[0]
    out_ref[...] = total([half_ref[...]] + [part[-more:, :] for part in parts]).astype(out_ref.dtype)


def half_sum(half, parts):
    return pl.pallas_call(
        half_kernel,
        out_shape=jax.ShapeDtypeStruct(half.shape, BF16),
        in_specs=[vmem()] * (1 + len(parts)),
        out_specs=vmem(),
        compiler_params=params(),
        cost_estimate=pl.CostEstimate(flops=half.size * 4, bytes_accessed=half.size * 12, transcendentals=0),
    )(half, *parts)


def last_kernel(weight_ref, own_ref, *refs):
    parts, out_ref = refs[:-1], refs[-1]
    block = own_ref.shape[0]
    rows = total([own_ref[...]] + [part[:block, :] for part in parts]).astype(BF16)
    out_ref[...] = lax.dot_general(
        rows, weight_ref[...], (((1,), (1,)), ((), ())), preferred_element_type=F32
    ).astype(out_ref.dtype)


def last_product(weight, own, parts):
    return pl.pallas_call(
        last_kernel,
        out_shape=jax.ShapeDtypeStruct(own.shape, BF16),
        in_specs=[vmem()] * (2 + len(parts)),
        out_specs=vmem(),
        compiler_params=params(),
        cost_estimate=pl.CostEstimate(flops=2 * own.size * own.shape[1], bytes_accessed=own.size * 12, transcendentals=0),
    )(weight, own, *parts)


def gather(value, order):
    return [value] + [send(value, "rep", at(d)) for d in order]


def join(mine):
    other = send(mine, "blk", at(1))
    is_first = lax.axis_index("blk") % 2 == 0
    return jnp.where(
        is_first, jnp.concatenate([mine, other], axis=0), jnp.concatenate([other, mine], axis=0)
    )


def shards_direct(features, weight, cotangent, rows, counts, tiles):
    block = features.shape[0]
    slabs, subs = lax.axis_size("blk"), lax.axis_size("rep")
    far, near, early = far_steps(slabs), sub_order(subs), [3, 2, 1] if subs == 4 else [1]
    straight = list(range(subs))
    order = [([0] + early).index(d) for d in [0] + near]
    node_count = block * slabs * subs
    even = far[:1] + [at(0)] + far[1:]
    odd = [lambda i, step=step: step(i) ^ 1 for step in even]
    dense = dense_adjacency(even + odd, [0] + near, rows, counts, tiles)

    pieces, dense = lax.optimization_barrier((gather(features, early), dense))
    other = send(apply_first(dense, pieces, order), "blk", at(1))
    rest, mine = apply_rest(dense, pieces, order, block)
    rest, other = lax.optimization_barrier((rest, other))
    (first,) = first_sum(mine, other, block)
    own, *sums = rest_sums(mine, send(rest, "blk", at(1)), block)
    parts = [send(value, "blk", step) for value, step in zip([first] + sums, far)]

    pair = layer([own] + parts, weight, cotangent)
    pairs = gather(pair, near)
    activation = layer_output(pair, weight)
    pairs[-1], activation = lax.optimization_barrier((pairs[-1], activation))
    cut, distances = subs // 2, [0] + near
    early_terms = apply_early(dense, pairs[:cut], distances[:cut])
    first, keep = apply_late(
        dense, early_terms, pairs[cut:], distances[cut:], 1.0 / math.sqrt(node_count)
    )
    other = send(first, "blk", at(1))
    rest, mine = apply_rest(dense, pairs, straight, block)
    rest, other = lax.optimization_barrier((rest, other))
    first, half = first_sum(mine, other, block, keep)
    own, *sums = rest_sums(mine, send(rest, "blk", at(1)), block, half)
    parts = [send(value, "blk", step) for value, step in zip([first] + sums, far)]
    grad = join(half_sum(half, parts)).astype(F32)
    return activation, grad, last_product(weight, own, parts)


def add_tile(running, column_block, node_slab, tiles, slot_rows, slot_counts):
    block_size = node_slab.shape[0]
    tile_now = lax.dynamic_index_in_dim(tiles, column_block, 0, keepdims=False)
    rows_now = lax.dynamic_index_in_dim(slot_rows, column_block, 0, keepdims=False)
    count_now = lax.dynamic_index_in_dim(slot_counts, column_block, 0, keepdims=False)

    def one_slot(slot_index, carried):
        weights_now = lax.dynamic_slice_in_dim(tile_now, slot_index * block_size, block_size, 1)
        product = jnp.dot(weights_now, node_slab, preferred_element_type=F32)
        first_row = rows_now[slot_index] * block_size
        current = lax.dynamic_slice_in_dim(carried, first_row, block_size, 0)
        return lax.dynamic_update_slice_in_dim(carried, current + product, first_row, 0)

    return lax.fori_loop(0, count_now, one_slot, running)


def aggregate(node_slab, tiles, slot_rows, slot_counts):
    block_size = node_slab.shape[0]
    running = jnp.zeros((block_size * lax.axis_size("rep"), node_slab.shape[1]), F32)
    piece = lax.all_gather(node_slab, "blk", axis=0, tiled=True)
    piece_count = piece.shape[0] // block_size

    def one_piece(inner, running_now):
        slab_now = lax.dynamic_slice_in_dim(piece, inner * block_size, block_size, 0)
        return add_tile(running_now, inner, slab_now, tiles, slot_rows, slot_counts)

    total = lax.fori_loop(0, piece_count, one_piece, running)
    return lax.psum_scatter(total.astype(BF16), "rep", scatter_dimension=0, tiled=True)


def shards_general(features, weight, cotangent, rows, counts, tiles):
    agg = aggregate(features, tiles, rows, counts)
    pre = jnp.dot(agg, weight, preferred_element_type=F32)
    sig = jax.nn.sigmoid(pre)
    activation = (pre * sig).astype(BF16)
    dpre = (cotangent.astype(F32) * sig * (1.0 + pre * (1.0 - sig))).astype(BF16)
    local_grad = lax.dot_general(agg, dpre, (((0,), (0,)), ((), ())), preferred_element_type=F32)
    node_count = features.shape[0] * lax.axis_size("blk") * lax.axis_size("rep")
    grad_weight = lax.psum(local_grad, ("blk", "rep")) / math.sqrt(node_count)
    back = lax.dot_general(dpre, weight, (((1,), (1,)), ((), ())), preferred_element_type=F32)
    return activation, grad_weight, aggregate(back.astype(BF16), tiles, rows, counts)


def shards(features, weight, cotangent, block_rows, block_counts, block_values):
    tiles = block_values[0, :, 0]
    rows = block_rows[0, :, 0]
    counts = block_counts[0, :, 0]
    sizes = lax.axis_size("blk"), lax.axis_size("rep")
    direct = sizes[0] in (4, 8) and sizes[1] in (2, 4)
    return (shards_direct if direct else shards_general)(
        features, weight, cotangent, rows, counts, tiles
    )


def solution(mesh):
    placed = (
        P(("blk", "rep"), None),
        P(),
        P(("blk", "rep"), None),
        P("blk", None, "rep", None),
        P("blk", None, "rep"),
        P("blk", None, "rep", None, None),
    )
    return jax.shard_map(
        shards,
        mesh=mesh,
        in_specs=placed,
        out_specs=(P(("blk", "rep"), None), P(), P(("blk", "rep"), None)),
        check_vma=False,
    )
```

```python
import functools
import math

import jax
import jax.numpy as jnp
from jax import lax
from jax.experimental import pallas as pl
from jax.experimental.pallas import tpu as pltpu
from jax.sharding import PartitionSpec as P

F32 = jnp.float32
BF16 = jnp.bfloat16
ROWS = (((0,), (0,)), ((), ()))
VMEM_LIMIT = 8 * 1024 * 1024


def vmem():
    return pl.BlockSpec(memory_space=pltpu.VMEM)


def smem():
    return pl.BlockSpec(memory_space=pltpu.SMEM)


def params():
    return pltpu.CompilerParams(vmem_limit_bytes=VMEM_LIMIT)


def send(value, axis, step):
    return lax.ppermute(value, axis, [(i, step(i)) for i in range(lax.axis_size(axis))])


def at(distance):
    return lambda i: i ^ distance


def far_steps(slabs):
    if slabs == 8:
        return [at(6), at(2), at(4)]
    return [at(2)]


def sub_order(subs):
    return [1, 3, 2] if subs == 4 else [1]


def dense_kernel(steps, subs, rows_ref, counts_ref, tiles_ref, out_ref):
    me, mine = lax.axis_index("blk"), lax.axis_index("rep")
    block = tiles_ref.shape[1]
    slots = tiles_ref.shape[2] // block
    for q, step in enumerate(steps):
        slab = step(me)
        tile = tiles_ref[slab]
        turned = [tile[:, k * block : (k + 1) * block].T for k in range(slots)]
        places = [
            jnp.where(k < counts_ref[slab], rows_ref[slab, k] ^ mine, -1) for k in range(slots)
        ]
        for b, sub in enumerate(subs):
            value = jnp.zeros((block, block), tile.dtype)
            for k in range(slots):
                value = jnp.where(places[k] == sub, turned[k], value)
            out_ref[q * block : (q + 1) * block, b * block : (b + 1) * block] = value


def dense_adjacency(steps, subs, rows, counts, tiles):
    block = tiles.shape[1]
    shape = (len(steps) * block, len(subs) * block)
    return pl.pallas_call(
        functools.partial(dense_kernel, steps, subs),
        out_shape=jax.ShapeDtypeStruct(shape, tiles.dtype),
        in_specs=[smem(), smem(), vmem()],
        out_specs=vmem(),
        compiler_params=params(),
        cost_estimate=pl.CostEstimate(flops=0, bytes_accessed=4 * tiles.size * 2, transcendentals=0),
    )(rows, counts, tiles)


def first_kernel(blocks, n_added, dense_ref, *refs):
    added, pieces, out_ref = refs[:n_added], refs[n_added:-1], refs[-1]
    block = out_ref.shape[0]
    rows = dense_ref.shape[0] // 2
    nodes = jnp.concatenate([piece[...] for piece in pieces], axis=0)
    columns = [dense_ref[rows : rows + block, k * block : (k + 1) * block] for k in blocks]
    product = jnp.dot(jnp.concatenate(columns, axis=1), nodes, preferred_element_type=F32)
    for more in added:
        product = more[...] + product
    out_ref[...] = product.astype(out_ref.dtype)


def apply_first(dense, pieces, order, kind, *added):
    shape = pieces[0].shape
    return pl.pallas_call(
        functools.partial(first_kernel, order, len(added)),
        out_shape=jax.ShapeDtypeStruct(shape, kind),
        in_specs=[vmem()] * (1 + len(added) + len(pieces)),
        out_specs=vmem(),
        compiler_params=params(),
        cost_estimate=pl.CostEstimate(
            flops=2 * len(pieces) * shape[0] * shape[0] * shape[1], bytes_accessed=dense.size // 4, transcendentals=0
        ),
    )(dense, *added, *pieces)


def rest_kernel(block, order, dense_ref, *refs):
    nodes = jnp.concatenate([refs[k][-block:, :] for k in order], axis=0)
    odd_ref, even_ref = refs[len(order) :]
    half = dense_ref.shape[0] // 2
    rows = dense_ref[dense_ref.shape[0] - odd_ref.shape[0] :, :]
    odd_ref[...] = jnp.dot(rows, nodes, preferred_element_type=F32).astype(odd_ref.dtype)
    even_ref[...] = jnp.dot(dense_ref[:half, :], nodes, preferred_element_type=F32)


def apply_rest(dense, pieces, order, block):
    rows, feat = dense.shape[0] // 2, pieces[0].shape[1]
    return pl.pallas_call(
        functools.partial(rest_kernel, block, order),
        out_shape=[jax.ShapeDtypeStruct((rows - block, feat), BF16), jax.ShapeDtypeStruct((rows, feat), F32)],
        in_specs=[vmem()] * (1 + len(pieces)),
        out_specs=[vmem()] * 2,
        compiler_params=params(),
        cost_estimate=pl.CostEstimate(
            flops=2 * dense.size * feat, bytes_accessed=2 * dense.size, transcendentals=0
        ),
    )(dense, *pieces)


def first_sum_kernel(even_ref, other_ref, *refs):
    block = even_ref.shape[0]
    if len(refs) == 1:
        refs[0][...] = (even_ref[...] + other_ref[...].astype(F32)).astype(BF16)
        return
    keep_ref, out_ref, half_ref = refs
    out_ref[:block, :] = (even_ref[...] + other_ref[:block, :].astype(F32)).astype(BF16)
    half = (keep_ref[...] + other_ref[block:, :].astype(F32)).astype(BF16)
    out_ref[block:, :] = half
    half_ref[...] = half


def first_sum(even, other, block, *keep):
    shapes = [jax.ShapeDtypeStruct(other.shape, BF16)]
    shapes += [jax.ShapeDtypeStruct(half.shape, BF16) for half in keep]
    top = pl.BlockSpec((block, even.shape[1]), lambda i: (0, 0))
    return pl.pallas_call(
        first_sum_kernel,
        grid=(1,),
        out_shape=shapes,
        in_specs=[top] + [vmem()] * (1 + len(keep)),
        out_specs=[vmem()] * len(shapes),
        compiler_params=params(),
        cost_estimate=pl.CostEstimate(flops=other.size, bytes_accessed=other.size * 8, transcendentals=0),
    )(even, other, *keep)


def rest_sum_kernel(n_half, even_ref, other_ref, *refs):
    half, (own_ref, *outs) = refs[:n_half], refs[n_half:]
    block = own_ref.shape[0]
    for q, out in enumerate([own_ref] + outs):
        both = even_ref[(q + 1) * block : (q + 2) * block, :]
        both = both + other_ref[q * block : (q + 1) * block, :].astype(F32)
        out[:block, :] = both.astype(out.dtype)
        if half and q:
            out[block:, :] = half[0][...]


def rest_sums(even, other, block, *half):
    feat = even.shape[1]
    more = half[0].shape[0] if half else 0
    n_out = other.shape[0] // block - 1
    shapes = [jax.ShapeDtypeStruct((block, feat), F32)]
    shapes += [jax.ShapeDtypeStruct((block + more, feat), BF16)] * n_out
    return pl.pallas_call(
        functools.partial(rest_sum_kernel, len(half)),
        out_shape=shapes,
        in_specs=[vmem()] * (2 + len(half)),
        out_specs=[vmem()] * len(shapes),
        compiler_params=params(),
        cost_estimate=pl.CostEstimate(flops=other.size, bytes_accessed=other.size * 8, transcendentals=0),
    )(even, other, *half)


def total(values):
    values = [value.astype(F32) for value in values]
    if len(values) == 2:
        return values[0] + values[1]
    mine, across, one, other = values
    return (mine + across) + (one + other)


def layer_kernel(n_parts, *refs):
    parts, (weight_ref, cotangent_ref, pair_ref) = refs[:n_parts], refs[n_parts:]
    block = cotangent_ref.shape[0]
    agg = total([part[...] for part in parts]).astype(BF16)
    pre = jnp.dot(agg, weight_ref[...], preferred_element_type=F32)
    sig = 1.0 / (1.0 + jnp.exp(-pre))
    dpre = cotangent_ref[...].astype(F32) * sig * (1.0 + pre * (1.0 - sig))
    pair_ref[:block, :] = agg
    pair_ref[block:, :] = dpre.astype(BF16)


def layer(parts, weight, cotangent):
    block, feat = cotangent.shape
    return pl.pallas_call(
        functools.partial(layer_kernel, len(parts)),
        out_shape=jax.ShapeDtypeStruct((2 * block, feat), BF16),
        in_specs=[vmem()] * (len(parts) + 2),
        out_specs=vmem(),
        compiler_params=params(),
        cost_estimate=pl.CostEstimate(
            flops=2 * block * feat * feat, bytes_accessed=block * feat * 16, transcendentals=block * feat
        ),
    )(*parts, weight, cotangent)


def activation_kernel(pair_ref, weight_ref, out_ref):
    pre = jnp.dot(pair_ref[: out_ref.shape[0], :], weight_ref[...], preferred_element_type=F32)
    out_ref[...] = (pre / (1.0 + jnp.exp(-pre))).astype(out_ref.dtype)


def layer_output(pair, weight):
    shape = (pair.shape[0] // 2, pair.shape[1])
    return pl.pallas_call(
        activation_kernel,
        out_shape=jax.ShapeDtypeStruct(shape, BF16),
        in_specs=[vmem()] * 2,
        out_specs=vmem(),
        compiler_params=params(),
        cost_estimate=pl.CostEstimate(
            flops=pair.size * shape[1], bytes_accessed=pair.size * 4, transcendentals=pair.size // 2
        ),
    )(pair, weight)


def pair_terms(dense, distances, pairs):
    block = pairs[0].shape[0] // 2
    first = jnp.dot(
        dense, jnp.concatenate([pair[block:, :] for pair in pairs], axis=0), preferred_element_type=F32
    )
    if len(pairs) == 2:
        mine = lax.axis_index("rep")
        flip = (mine ^ distances[0]) > (mine ^ distances[1])
        one, two = pairs
        pairs = [jnp.where(flip, two, one), jnp.where(flip, one, two)]
    agg = jnp.concatenate([pair[:block, :] for pair in pairs], axis=0)
    dpre = jnp.concatenate([pair[block:, :] for pair in pairs], axis=0)
    return first, lax.dot_general(agg, dpre, ROWS, preferred_element_type=F32)


def early_kernel(distances, dense_ref, *refs):
    pairs, (first_ref, grad_ref) = refs[: len(distances)], refs[len(distances) :]
    block = first_ref.shape[0]
    rows = dense_ref.shape[0] // 2
    part = dense_ref[rows : rows + block, : len(pairs) * block]
    first_ref[...], grad_ref[...] = pair_terms(part, distances, [pair[...] for pair in pairs])


def late_kernel(scale, distances, dense_ref, early_ref, grad_ref, *refs):
    pairs, (first_ref, keep_ref) = refs[: len(distances)], refs[len(distances) :]
    block = early_ref.shape[0]
    rows, columns = dense_ref.shape[0] // 2, dense_ref.shape[1] - len(pairs) * block
    part = dense_ref[rows : rows + block, columns:]
    first, grad = pair_terms(part, distances, [pair[...] for pair in pairs])
    first_ref[:block, :] = (early_ref[...] + first).astype(BF16)
    grad = (grad_ref[...] + grad) * scale
    half = grad.shape[0] // 2
    upper, lower = grad[:half, :], grad[half:, :]
    is_first = lax.axis_index("blk") % 2 == 0
    first_ref[block:, :] = jnp.where(is_first, lower, upper).astype(BF16)
    keep_ref[...] = jnp.where(is_first, upper, lower)


def apply_early(dense, pairs, distances):
    block, feat = pairs[0].shape[0] // 2, pairs[0].shape[1]
    return pl.pallas_call(
        functools.partial(early_kernel, distances),
        out_shape=[jax.ShapeDtypeStruct((n, feat), F32) for n in (block, feat)],
        in_specs=[vmem()] * (1 + len(pairs)),
        out_specs=[vmem()] * 2,
        compiler_params=params(),
        cost_estimate=pl.CostEstimate(
            flops=6 * len(pairs) * block * feat * feat, bytes_accessed=dense.size, transcendentals=0
        ),
    )(dense, *pairs)


def apply_late(dense, early, pairs, distances, scale):
    feat = pairs[0].shape[1]
    block, half = pairs[0].shape[0] // 2, feat // 2
    shapes = ((block + half, BF16), (half, F32))
    return pl.pallas_call(
        functools.partial(late_kernel, scale, distances),
        out_shape=[jax.ShapeDtypeStruct((n, feat), t) for n, t in shapes],
        in_specs=[vmem()] * (3 + len(pairs)),
        out_specs=[vmem()] * 2,
        compiler_params=params(),
        cost_estimate=pl.CostEstimate(
            flops=6 * len(pairs) * block * feat * feat, bytes_accessed=dense.size, transcendentals=0
        ),
    )(dense, *early, *pairs)


def half_kernel(half_ref, *refs):
    parts, out_ref = refs[:-1], refs[-1]
    more = half_ref.shape[0]
    out_ref[...] = total([half_ref[...]] + [part[-more:, :] for part in parts]).astype(out_ref.dtype)


def half_sum(half, parts):
    return pl.pallas_call(
        half_kernel,
        out_shape=jax.ShapeDtypeStruct(half.shape, BF16),
        in_specs=[vmem()] * (1 + len(parts)),
        out_specs=vmem(),
        compiler_params=params(),
        cost_estimate=pl.CostEstimate(flops=half.size * 4, bytes_accessed=half.size * 12, transcendentals=0),
    )(half, *parts)


def last_kernel(weight_ref, own_ref, *refs):
    parts, out_ref = refs[:-1], refs[-1]
    block = own_ref.shape[0]
    rows = total([own_ref[...]] + [part[:block, :] for part in parts]).astype(BF16)
    out_ref[...] = lax.dot_general(
        rows, weight_ref[...], (((1,), (1,)), ((), ())), preferred_element_type=F32
    ).astype(out_ref.dtype)


def last_product(weight, own, parts):
    return pl.pallas_call(
        last_kernel,
        out_shape=jax.ShapeDtypeStruct(own.shape, BF16),
        in_specs=[vmem()] * (2 + len(parts)),
        out_specs=vmem(),
        compiler_params=params(),
        cost_estimate=pl.CostEstimate(flops=2 * own.size * own.shape[1], bytes_accessed=own.size * 12, transcendentals=0),
    )(weight, own, *parts)


def gather(value, order):
    return [value] + [send(value, "rep", at(d)) for d in order]


def join(mine):
    other = send(mine, "blk", at(1))
    is_first = lax.axis_index("blk") % 2 == 0
    return jnp.where(
        is_first, jnp.concatenate([mine, other], axis=0), jnp.concatenate([other, mine], axis=0)
    )


def shards_direct(features, weight, cotangent, rows, counts, tiles):
    block = features.shape[0]
    slabs, subs = lax.axis_size("blk"), lax.axis_size("rep")
    far, near, early = far_steps(slabs), sub_order(subs), [3, 2, 1] if subs == 4 else [1]
    straight = list(range(subs))
    order = [([0] + early).index(d) for d in [0] + near]
    node_count = block * slabs * subs
    even = far[:1] + [at(0)] + far[1:]
    odd = [lambda i, step=step: step(i) ^ 1 for step in even]
    dense = dense_adjacency(even + odd, [0] + near, rows, counts, tiles)

    pieces = gather(features, early)
    places = [([0] + near).index(d) for d in [0] + early]
    cut = subs // 2
    first = apply_first(dense, pieces[:cut], places[:cut], F32)
    first = apply_first(dense, pieces[cut:], places[cut:], BF16, first)
    other = send(first, "blk", at(1))
    rest, mine = apply_rest(dense, pieces, order, block)
    rest, other = lax.optimization_barrier((rest, other))
    (first,) = first_sum(mine, other, block)
    own, *sums = rest_sums(mine, send(rest, "blk", at(1)), block)
    parts = [send(value, "blk", step) for value, step in zip([first] + sums, far)]

    pair = layer([own] + parts, weight, cotangent)
    pairs = gather(pair, near)
    activation = layer_output(pair, weight)
    pairs[-1], activation = lax.optimization_barrier((pairs[-1], activation))
    distances = [0] + near
    early_terms = apply_early(dense, pairs[:cut], distances[:cut])
    first, keep = apply_late(
        dense, early_terms, pairs[cut:], distances[cut:], 1.0 / math.sqrt(node_count)
    )
    other = send(first, "blk", at(1))
    rest, mine = apply_rest(dense, pairs, straight, block)
    rest, other = lax.optimization_barrier((rest, other))
    first, half = first_sum(mine, other, block, keep)
    own, *sums = rest_sums(mine, send(rest, "blk", at(1)), block, half)
    parts = [send(value, "blk", step) for value, step in zip([first] + sums, far)]
    grad = join(half_sum(half, parts)).astype(F32)
    return activation, grad, last_product(weight, own, parts)


def add_tile(running, column_block, node_slab, tiles, slot_rows, slot_counts):
    block_size = node_slab.shape[0]
    tile_now = lax.dynamic_index_in_dim(tiles, column_block, 0, keepdims=False)
    rows_now = lax.dynamic_index_in_dim(slot_rows, column_block, 0, keepdims=False)
    count_now = lax.dynamic_index_in_dim(slot_counts, column_block, 0, keepdims=False)

    def one_slot(slot_index, carried):
        weights_now = lax.dynamic_slice_in_dim(tile_now, slot_index * block_size, block_size, 1)
        product = jnp.dot(weights_now, node_slab, preferred_element_type=F32)
        first_row = rows_now[slot_index] * block_size
        current = lax.dynamic_slice_in_dim(carried, first_row, block_size, 0)
        return lax.dynamic_update_slice_in_dim(carried, current + product, first_row, 0)

    return lax.fori_loop(0, count_now, one_slot, running)


def aggregate(node_slab, tiles, slot_rows, slot_counts):
    block_size = node_slab.shape[0]
    running = jnp.zeros((block_size * lax.axis_size("rep"), node_slab.shape[1]), F32)
    piece = lax.all_gather(node_slab, "blk", axis=0, tiled=True)
    piece_count = piece.shape[0] // block_size

    def one_piece(inner, running_now):
        slab_now = lax.dynamic_slice_in_dim(piece, inner * block_size, block_size, 0)
        return add_tile(running_now, inner, slab_now, tiles, slot_rows, slot_counts)

    total = lax.fori_loop(0, piece_count, one_piece, running)
    return lax.psum_scatter(total.astype(BF16), "rep", scatter_dimension=0, tiled=True)


def shards_general(features, weight, cotangent, rows, counts, tiles):
    agg = aggregate(features, tiles, rows, counts)
    pre = jnp.dot(agg, weight, preferred_element_type=F32)
    sig = jax.nn.sigmoid(pre)
    activation = (pre * sig).astype(BF16)
    dpre = (cotangent.astype(F32) * sig * (1.0 + pre * (1.0 - sig))).astype(BF16)
    local_grad = lax.dot_general(agg, dpre, (((0,), (0,)), ((), ())), preferred_element_type=F32)
    node_count = features.shape[0] * lax.axis_size("blk") * lax.axis_size("rep")
    grad_weight = lax.psum(local_grad, ("blk", "rep")) / math.sqrt(node_count)
    back = lax.dot_general(dpre, weight, (((1,), (1,)), ((), ())), preferred_element_type=F32)
    return activation, grad_weight, aggregate(back.astype(BF16), tiles, rows, counts)


def shards(features, weight, cotangent, block_rows, block_counts, block_values):
    tiles = block_values[0, :, 0]
    rows = block_rows[0, :, 0]
    counts = block_counts[0, :, 0]
    sizes = lax.axis_size("blk"), lax.axis_size("rep")
    direct = sizes[0] in (4, 8) and sizes[1] in (2, 4)
    return (shards_direct if direct else shards_general)(
        features, weight, cotangent, rows, counts, tiles
    )


def solution(mesh):
    placed = (
        P(("blk", "rep"), None),
        P(),
        P(("blk", "rep"), None),
        P("blk", None, "rep", None),
        P("blk", None, "rep"),
        P("blk", None, "rep", None, None),
    )
    return jax.shard_map(
        shards,
        mesh=mesh,
        in_specs=placed,
        out_specs=(P(("blk", "rep"), None), P(), P(("blk", "rep"), None)),
        check_vma=False,
    )
```
